32 devices in a mesh: groups: 2 (over y), ctx: 4 (over z), head: 2 (over x), pair: 2 (over core).
Axes of the slice: x: 2, y: 2, z: 4, core: 2. Of those that a mesh axis runs over, the one named last changes fastest.
Arguments:
- student_query: bfloat16 [1024, 4096], P(('groups', 'ctx'), ('head', 'pair')), parts along dimension 0, may hold values from -25 to 25
- teacher_keys: bfloat16 [1024, 1024], P(('groups', 'ctx'), ('head', 'pair')), parts along dimension 0, may hold values from -9 to 9
- teacher_values: bfloat16 [1024, 1024], P(('groups', 'ctx'), ('head', 'pair')), parts along dimension 0, may hold values from -6 to 6
- band_span: int32 [1024], P(('groups', 'ctx')), parts along dimension 0, may hold values from 256 to 1024, as said below
- residual_in: bfloat16 [1024, 4096], P(('groups', 'ctx'), ('head', 'pair')), parts along dimension 0, may hold values from -3 to 3
- norm_gain: float32 [4096], replicated, may hold values from 0.25 to 1.75
- w_gate: bfloat16 [4096, 7168], P('ctx', ('head', 'pair')), may hold values from -0.09375 to 0.09375
- w_up: bfloat16 [4096, 7168], P('ctx', ('head', 'pair')), may hold values from -0.09375 to 0.09375
- w_down: bfloat16 [7168, 4096], P(('head', 'pair'), 'ctx'), may hold values from -0.0625 to 0.0625
- teacher_feats: bfloat16 [1024, 7168], P(('groups', 'ctx'), ('head', 'pair')), parts along dimension 0, may hold values from -31 to 31
- keep_tiles: int32 [1024, 56], P(('groups', 'ctx'), ('head', 'pair')), parts along dimension 0, may hold values from 0 to 1, as said below
Outputs:
- layer_out: bfloat16 [1024, 4096], P(('groups', 'ctx'), ('head', 'pair')), parts along dimension 0
- loss_value: float32 [2], P('groups'), parts along dimension 0
- grad_resid: float32 [1024, 4096], P(('groups', 'ctx'), ('head', 'pair')), parts along dimension 0
The draws below stay inside these ranges and needn't reach their ends.
There are 2 independent parts, one for each index of `groups`. The reference program is written for one: setup_inputs(seed, part) draws one part's arguments, and reference() takes and returns one part's arrays. A program takes and returns all parts, laid end to end along the dimension named above; an argument that names none is the same for every part. Nothing has to cross between parts.
Inputs may be any that keep to these rules, and one draw needn't show every extreme that they name: `band_span`: some token's span equals 1024. `keep_tiles`: the first token keeps every tile.
All inputs are finite; a program needn't handle non-finite values.
Results may differ from the reference program's by a relative error of at most 0.014.
Values may be sent and summed in bfloat16 or wider, within the bound.
A program may use at most 128 MiB of HBM per device.

```python
import math
import jax
import jax.numpy as jnp
from jax import lax

D = 4096
HEADS = 32
KV_HEADS = 8
HEAD_DIM = 128
FF = 7168
TILE = 128
TOKENS = 512
WINDOW = 1024
GROUP_FF = 1792


def teacher_key_rows(key):
    drawn_keys = jnp.clip(2.0 * jax.random.normal(jax.random.fold_in(key, 101), (TOKENS, KV_HEADS * HEAD_DIM), jnp.float32), -9.0, 9.0)
    return drawn_keys


def draw_teacher_keys(key, part):
    return teacher_key_rows(key).astype(jnp.bfloat16)


def draw_student_query(key, part):
    drawn_query = jnp.clip(jax.random.normal(jax.random.fold_in(key, 7), (TOKENS, D), jnp.float32), -6.0, 6.0)
    return drawn_query.astype(jnp.bfloat16)


def draw_teacher_feats(key, part):
    spread = math.log(10.0)
    row_scale = jnp.exp(jax.random.uniform(jax.random.fold_in(key, 21), (TOKENS, 1), jnp.float32, 0.0, spread)) / math.sqrt(10.0)
    col_scale = jnp.exp(jax.random.uniform(jax.random.fold_in(key, 22), (1, FF), jnp.float32, 0.0, spread)) / math.sqrt(10.0)
    noise_field = jnp.clip(jax.random.normal(jax.random.fold_in(key, 23), (TOKENS, FF), jnp.float32), -6.0, 6.0)
    drawn_feats = 0.5 * noise_field * row_scale * col_scale
    return drawn_feats.astype(jnp.bfloat16)


def draw_keep_tiles(key, part):
    positions = jnp.arange(TOKENS, dtype=jnp.int32)
    threshold = 250 + 500 * positions // max(TOKENS - 1, 1)
    rolled = jax.random.randint(jax.random.fold_in(key, 31), (TOKENS, FF // TILE), 0, 1000, dtype=jnp.int32)
    keep_drawn = (rolled < threshold[:, None]).astype(jnp.int32)
    return keep_drawn.at[0].set(1)


def draw_band_span(key, part):
    spans_drawn = jax.random.randint(jax.random.fold_in(key, 41), (TOKENS,), WINDOW // 4, WINDOW + 1, dtype=jnp.int32)
    return spans_drawn.at[TOKENS - 1].set(WINDOW)


def shard_levels(own_key, dims, cuts, smallest, high):
    gain = 1.0
    for axis_at, shards_of in cuts:
        draws = jax.random.uniform(jax.random.fold_in(jax.random.fold_in(own_key, 6), axis_at), (shards_of,), jnp.float32, smallest / len(cuts), high / len(cuts))
        gain = gain * jnp.repeat(jnp.exp(draws), dims[axis_at] // shards_of).reshape((-1,) + (1,) * (len(dims) - 1 - axis_at))
    return gain


def bell_draw(key, dims, width, reach, shards=(), kind=jnp.bfloat16):
    factor_of = shard_levels(key, dims, shards, -0.22, 0.18) if shards else 1.0
    drawn = jax.random.normal(key, dims, jnp.float32) * width * factor_of
    return jnp.minimum(jnp.maximum(drawn, -reach), reach).astype(kind)


def setup_inputs(seed: int = 0, part: int = 0) -> dict:
    key_list = jax.random.split(jax.random.key(seed), 12)
    own_keys = jax.random.split(jax.random.fold_in(key_list[11], part), 12)
    return {
        "student_query": draw_student_query(jax.random.fold_in(jax.random.fold_in(key_list[11], part), 71), part),
        "teacher_keys": draw_teacher_keys(jax.random.fold_in(jax.random.fold_in(key_list[11], part), 71), part),
        "teacher_values": bell_draw(own_keys[2], (TOKENS, KV_HEADS * HEAD_DIM), 1.0, 6.0, ((0, 4), (1, 4))),
        "band_span": draw_band_span(jax.random.fold_in(jax.random.fold_in(key_list[11], part), 71), part),
        "residual_in": bell_draw(own_keys[4], (TOKENS, D), 0.5, 3.0, ((0, 4), (1, 4))),
        "norm_gain": jnp.clip(1.0 + 0.15 * jax.random.normal(key_list[5], (D,), jnp.float32), 0.25, 1.75),
        "w_gate": bell_draw(key_list[6], (D, FF), D ** -0.5, 0.09375, ((0, 4), (1, 4))),
        "w_up": bell_draw(key_list[7], (D, FF), D ** -0.5, 0.09375, ((0, 4), (1, 4))),
        "w_down": bell_draw(key_list[8], (FF, D), FF ** -0.5, 0.0625, ((0, 4), (1, 4))),
        "teacher_feats": draw_teacher_feats(jax.random.fold_in(jax.random.fold_in(key_list[11], part), 71), part),
        "keep_tiles": draw_keep_tiles(jax.random.fold_in(jax.random.fold_in(key_list[11], part), 71), part),
    }


def reference(student_query, teacher_keys, teacher_values, band_span, residual_in, norm_gain, w_gate, w_up, w_down, teacher_feats, keep_tiles):
    group_size = HEADS // KV_HEADS
    query_block = math.gcd(TOKENS, 512)
    span_length = WINDOW + query_block
    keys_padded = jnp.pad(teacher_keys, ((WINDOW, 0), (0, 0)))
    values_padded = jnp.pad(teacher_values, ((WINDOW, 0), (0, 0)))
    score_scale = 1.0 / math.sqrt(HEAD_DIM)

    def one_block(block_index):
        first_row = block_index * query_block
        query_rows = lax.dynamic_slice_in_dim(student_query, first_row, query_block, 0)
        query_rows = query_rows.astype(jnp.float32).reshape(query_block, KV_HEADS, group_size, HEAD_DIM)
        key_rows = lax.dynamic_slice_in_dim(keys_padded, first_row, span_length, 0)
        key_rows = key_rows.astype(jnp.float32).reshape(span_length, KV_HEADS, HEAD_DIM)
        value_rows = lax.dynamic_slice_in_dim(values_padded, first_row, span_length, 0)
        value_rows = value_rows.astype(jnp.float32).reshape(span_length, KV_HEADS, HEAD_DIM)
        spans_here = lax.dynamic_slice_in_dim(band_span, first_row, query_block, 0)
        query_pos = first_row + jnp.arange(query_block, dtype=jnp.int32)
        key_pos = first_row - WINDOW + jnp.arange(span_length, dtype=jnp.int32)
        distance = query_pos[:, None] - key_pos[None, :]
        allowed = (distance >= 0) & (distance < spans_here[:, None]) & (key_pos[None, :] >= 0)
        scores = jnp.einsum('tkgd,skd->kgts', query_rows, key_rows) * score_scale
        masked = jnp.where(allowed[None, None], scores, -jnp.inf)
        highest = lax.optimization_barrier(jnp.max(masked, axis=-1, keepdims=True))
        weights = jnp.exp(masked - highest)
        normalized = (weights / lax.optimization_barrier(jnp.sum(weights, axis=-1, keepdims=True))).astype(jnp.bfloat16)
        mixed_rows = jnp.einsum('kgts,skd->tkgd', normalized.astype(jnp.float32), value_rows)
        return mixed_rows.reshape(query_block, D)
    attended = lax.map(one_block, jnp.arange(TOKENS // query_block, dtype=jnp.int32)).reshape(TOKENS, D)
    resid = (residual_in.astype(jnp.float32) + attended).astype(jnp.bfloat16)
    resid_float = resid.astype(jnp.float32)
    rms_value = jnp.sqrt(lax.optimization_barrier(jnp.mean(resid_float * resid_float, axis=1, keepdims=True)) + 1e-05)
    normed = (resid_float / rms_value * norm_gain).astype(jnp.bfloat16)
    gate_proj = jnp.dot(normed, w_gate, preferred_element_type=jnp.float32)
    up_proj = jnp.dot(normed, w_up, preferred_element_type=jnp.float32)
    lifted = jnp.maximum(gate_proj, 0.0)
    squared = lifted * lifted
    act_value = squared * up_proj
    hidden = act_value.astype(jnp.bfloat16)
    summed_out = resid_float
    for group_index in range(FF // GROUP_FF):
        first_col = group_index * GROUP_FF
        last_col = first_col + GROUP_FF
        group_term = jnp.dot(hidden[:, first_col:last_col], w_down[first_col:last_col, :], preferred_element_type=jnp.float32)
        summed_out = summed_out + group_term.astype(jnp.bfloat16).astype(jnp.float32)
    layer_out = summed_out.astype(jnp.bfloat16)
    keep_wide = jnp.repeat(keep_tiles.astype(jnp.float32), TILE, axis=1)
    differ = act_value - teacher_feats.astype(jnp.float32)
    kept_total = jnp.sum(keep_tiles.astype(jnp.float32)) * TILE
    loss_value = (jnp.sum(keep_wide * differ * differ) / kept_total).reshape(1)
    grad_act = keep_wide * differ
    grad_gate = (grad_act * up_proj * 2.0 * lifted).astype(jnp.bfloat16)
    grad_up = (grad_act * squared).astype(jnp.bfloat16)
    grad_norm = jnp.zeros((TOKENS, D), jnp.float32)
    for group_index in range(FF // GROUP_FF):
        first_col = group_index * GROUP_FF
        last_col = first_col + GROUP_FF
        group_term = jnp.dot(grad_gate[:, first_col:last_col], w_gate[:, first_col:last_col].T, preferred_element_type=jnp.float32)
        group_term = group_term + jnp.dot(grad_up[:, first_col:last_col], w_up[:, first_col:last_col].T, preferred_element_type=jnp.float32)
        grad_norm = grad_norm + group_term.astype(jnp.bfloat16).astype(jnp.float32)
    inner_sum = lax.optimization_barrier(jnp.sum(norm_gain * grad_norm * resid_float, axis=1, keepdims=True))
    grad_resid = norm_gain * grad_norm / rms_value - resid_float * inner_sum / (D * rms_value * rms_value * rms_value)
    return (layer_out, loss_value, grad_resid)
```

```python
import math

import jax
import jax.numpy as jnp
from jax import lax
from jax.sharding import PartitionSpec as P

D = 4096
HEADS = 32
KV_HEADS = 8
HEAD_DIM = 128
TILE = 128


def attend_heads(query_part, key_rows, value_rows, allowed):
    scores = jnp.einsum("thd,sd->hts", query_part, key_rows, preferred_element_type=jnp.float32) * (
        1.0 / math.sqrt(HEAD_DIM)
    )
    masked = jnp.where(allowed[None], scores, -jnp.inf)
    highest = jnp.max(masked, axis=-1, keepdims=True)
    weights = jnp.exp(masked - highest)
    normalized = (weights / jnp.sum(weights, axis=-1, keepdims=True)).astype(jnp.bfloat16)
    return jnp.einsum("hts,sd->thd", normalized, value_rows, preferred_element_type=jnp.float32)


def local(
    student_query,
    teacher_keys,
    teacher_values,
    band_span,
    residual_in,
    norm_gain,
    w_gate,
    w_up,
    w_down,
    teacher_feats,
    keep_tiles,
):
    tok_rows = student_query.shape[0]
    kv_local = teacher_keys.shape[1] // HEAD_DIM
    group_size = HEADS // KV_HEADS
    ctx_index = lax.axis_index("ctx")
    paired = jnp.concatenate([teacher_keys, teacher_values], axis=1)
    all_kv = lax.all_gather(paired, "ctx", axis=0, tiled=True)
    total_rows = all_kv.shape[0]
    key_pos = jnp.arange(total_rows, dtype=jnp.int32)
    query_pos = ctx_index * tok_rows + jnp.arange(tok_rows, dtype=jnp.int32)
    distance = query_pos[:, None] - key_pos[None, :]
    allowed = (distance >= 0) & (distance < band_span[:, None])
    keys_flat = all_kv[:, : kv_local * HEAD_DIM].reshape(total_rows, kv_local, HEAD_DIM)
    values_flat = all_kv[:, kv_local * HEAD_DIM :].reshape(total_rows, kv_local, HEAD_DIM)
    query_heads = student_query.reshape(tok_rows, kv_local, group_size, HEAD_DIM)
    outputs = []
    for kv_head in range(kv_local):
        for first_head in range(0, group_size, 2):
            outputs.append(
                attend_heads(
                    query_heads[:, kv_head, first_head : first_head + 2],
                    keys_flat[:, kv_head],
                    values_flat[:, kv_head],
                    allowed,
                )
            )
    attended = jnp.concatenate(outputs, axis=1).reshape(tok_rows, -1)
    residual = (residual_in.astype(jnp.float32) + attended).astype(jnp.bfloat16)
    resid_own = residual.astype(jnp.float32)
    square_sum = lax.psum(jnp.sum(resid_own * resid_own, axis=1, keepdims=True), ("head", "pair"))
    rms_value = jnp.sqrt(square_sum / D + 1e-05)
    own_cols = residual.shape[1]
    own_start = lax.axis_index(("head", "pair")) * own_cols
    gain_own = lax.dynamic_slice_in_dim(norm_gain, own_start, own_cols, 0)
    scaled = (resid_own * gain_own).astype(jnp.bfloat16)
    wide = lax.all_gather(scaled, ("head", "pair"), axis=1, tiled=True)
    rows = lax.all_to_all(wide, "ctx", split_axis=1, concat_axis=0, tiled=True)
    ff_local = w_gate.shape[1]
    partial = jnp.concatenate(
        [
            jnp.dot(rows, w_gate, preferred_element_type=jnp.float32).astype(jnp.bfloat16),
            jnp.dot(rows, w_up, preferred_element_type=jnp.float32).astype(jnp.bfloat16),
        ],
        axis=1,
    )
    both = lax.psum_scatter(partial, "ctx", scatter_dimension=0, tiled=True).astype(jnp.float32)
    both = both / rms_value
    gate_proj, up_proj = both[:, :ff_local], both[:, ff_local:]
    lifted = jnp.maximum(gate_proj, 0.0)
    squared = lifted * lifted
    act_value = squared * up_proj
    hidden = act_value.astype(jnp.bfloat16)
    tile_count = keep_tiles.shape[1]
    keep_float = keep_tiles.astype(jnp.float32)
    keep_wide = jnp.broadcast_to(keep_float[:, :, None], (tok_rows, tile_count, TILE)).reshape(
        tok_rows, tile_count * TILE
    )
    differ = act_value - teacher_feats.astype(jnp.float32)
    loss_part = jnp.sum(keep_wide * differ * differ)
    count_part = jnp.sum(keep_float) * TILE
    loss_total, count_total = lax.psum((loss_part, count_part), ("ctx", "head", "pair"))
    loss_value = (loss_total / count_total).reshape(1)
    grad_act = keep_wide * differ
    grad_gate = (grad_act * up_proj * 2.0 * lifted).astype(jnp.bfloat16)
    grad_up = (grad_act * squared).astype(jnp.bfloat16)
    all_hidden = lax.all_gather(hidden, "ctx", axis=0, tiled=True)
    all_gate = lax.all_gather(grad_gate, "ctx", axis=0, tiled=True)
    all_up = lax.all_gather(grad_up, "ctx", axis=0, tiled=True)
    contract = (((1,), (1,)), ((), ()))

    def own_sum(part):
        mine = lax.psum_scatter(
            part.astype(jnp.bfloat16), ("head", "pair"), scatter_dimension=1, tiled=True
        )
        byctx = lax.all_to_all(mine, "ctx", split_axis=0, concat_axis=0, tiled=True)
        blocks = lax.axis_size("ctx")
        width = byctx.shape[1]
        byctx = byctx.reshape(blocks, tok_rows, width)
        back = lax.all_to_all(byctx, ("head", "pair"), split_axis=0, concat_axis=2, tiled=True)
        return jnp.swapaxes(back, 0, 1).reshape(tok_rows, own_cols).astype(jnp.float32)

    down_sum = own_sum(jnp.dot(all_hidden, w_down, preferred_element_type=jnp.float32))
    layer_out = (resid_own + down_sum).astype(jnp.bfloat16)
    grad_part = lax.dot_general(all_gate, w_gate, contract, preferred_element_type=jnp.float32)
    grad_part = grad_part + lax.dot_general(
        all_up, w_up, contract, preferred_element_type=jnp.float32
    )
    grad_norm = own_sum(grad_part)
    rms_cubed = rms_value * rms_value * rms_value
    inner_sum = lax.psum(
        jnp.sum(gain_own * grad_norm * resid_own, axis=1, keepdims=True), ("head", "pair")
    )
    grad_resid = gain_own * grad_norm / rms_value - resid_own * inner_sum / (D * rms_cubed)
    return (layer_out, loss_value, grad_resid)


def solution(mesh):
    in_specs = (
        P(("groups", "ctx"), ("head", "pair")),
        P(("groups", "ctx"), ("head", "pair")),
        P(("groups", "ctx"), ("head", "pair")),
        P(("groups", "ctx")),
        P(("groups", "ctx"), ("head", "pair")),
        P(),
        P("ctx", ("head", "pair")),
        P("ctx", ("head", "pair")),
        P(("head", "pair"), "ctx"),
        P(("groups", "ctx"), ("head", "pair")),
        P(("groups", "ctx"), ("head", "pair")),
    )
    out_specs = (
        P(("groups", "ctx"), ("head", "pair")),
        P("groups"),
        P(("groups", "ctx"), ("head", "pair")),
    )
    return jax.shard_map(local, mesh=mesh, in_specs=in_specs, out_specs=out_specs, check_vma=False)
```

```python
import functools
import math

import jax
import jax.numpy as jnp
from jax import lax
from jax.experimental import pallas as pl
from jax.experimental.pallas import tpu as pltpu
from jax.sharding import PartitionSpec as P

HEAD_DIM = 128
TILE = 128
CHUNKS = 7
MESH = pl.DeviceIdType.MESH
F32 = jnp.float32
BF16 = jnp.bfloat16


def layer_kernel(
    nc, nhead, npair, chunks,
    q_ref, k_ref, v_ref, span_ref, res_ref, gain_ref, wg_hbm, wu_hbm, wd_hbm, feats_ref, keep_ref,
    out_ref, loss_ref, grad_ref,
    wg, wu, wd, kbuf, vbuf, resid, squares, nbuf, xall, tmp, part, fromleft, fromright, own,
    gathered, acc_down, acc_grad, keep_wide, sums, pair_in, head_in, final, inner, loss_head,
    loss_ctx, loss_acc,
    w_sem, kv_send, kv_recv, sq_send, sq_recv, n_send, n_recv, x_send, x_recv, rs_send, right_recv,
    left_recv, ag_send, ag_recv, p_send, p_recv, h_send, h_recv, f_send, f_recv, in_send, in_recv,
    lh_send, lh_recv, lc_send, lc_recv,
):
    nh = nhead * npair
    nb = nc // nh
    rows = q_ref.shape[0]
    sub = rows // nh
    dc = wg.shape[0]
    width = nc * dc
    ff = wg.shape[1]
    cw = ff // chunks
    c = lax.axis_index("ctx")
    my_head = lax.axis_index("head")
    my_pair = lax.axis_index("pair")
    h = my_head * npair + my_pair

    def remote(src, dst, send, recv, to_c, to_h):
        return pltpu.make_async_remote_copy(
            src_ref=src, dst_ref=dst, send_sem=send, recv_sem=recv,
            device_id={"ctx": to_c, "head": to_h // npair, "pair": to_h % npair},
            device_id_type=MESH,
        )

    weight_copies = [
        pltpu.make_async_copy(a, b, w_sem.at[i])
        for i, (a, b) in enumerate(((wg_hbm, wg), (wu_hbm, wu), (wd_hbm, wd)))
    ]
    for copy in weight_copies:
        copy.start()

    barrier = pltpu.get_barrier_semaphore()

    def greet(i, carry):
        to_c, to_h = i // nh, i % nh

        @pl.when((to_c != c) | (to_h != h))
        def _():
            pl.semaphore_signal(
                barrier, inc=1,
                device_id={"ctx": to_c, "head": to_h // npair, "pair": to_h % npair},
                device_id_type=MESH,
            )

        return carry

    lax.fori_loop(0, nc * nh, greet, 0)
    pl.semaphore_wait(barrier, nc * nh - 1)

    def kv_copies(block, to_c):
        return (
            remote(kbuf.at[block], kbuf.at[block], kv_send.at[0, to_c], kv_recv.at[0, block], to_c, h),
            remote(vbuf.at[block], vbuf.at[block], kv_send.at[1, to_c], kv_recv.at[1, block], to_c, h),
        )

    kbuf[c] = k_ref[...]
    vbuf[c] = v_ref[...]
    for other in range(nc):
        @pl.when(other > c)
        def _(other=other):
            for copy in kv_copies(c, other):
                copy.start()
            kbuf[other] = jnp.zeros_like(k_ref)
            vbuf[other] = jnp.zeros_like(v_ref)
    tile_count = keep_ref.shape[1]
    for t in range(tile_count):
        keep_wide[:, t * TILE : (t + 1) * TILE] = jnp.broadcast_to(
            keep_ref[:, t : t + 1].astype(F32), (rows, TILE)
        ).astype(BF16)
    for other in range(nc):
        @pl.when(other < c)
        def _(other=other):
            for copy in kv_copies(other, c):
                copy.wait_recv()

    span = nc * rows
    key_pos = lax.broadcasted_iota(jnp.int32, (rows, span), 1)
    query_pos = c * rows + lax.broadcasted_iota(jnp.int32, (rows, span), 0)
    distance = query_pos - key_pos
    allowed = (distance >= 0) & (distance < span_ref[...])
    kv_heads = k_ref.shape[1] // HEAD_DIM
    heads = q_ref.shape[1] // HEAD_DIM
    per = heads // kv_heads
    for kv in range(kv_heads):
        kcols = slice(kv * HEAD_DIM, (kv + 1) * HEAD_DIM)
        keys = kbuf[:, :, kcols].reshape(span, HEAD_DIM)
        values = vbuf[:, :, kcols].reshape(span, HEAD_DIM)
        for a in range(kv * per, (kv + 1) * per):
            cols = slice(a * HEAD_DIM, (a + 1) * HEAD_DIM)
            scores = lax.dot_general(
                q_ref[:, cols], keys, (((1,), (1,)), ((), ())), preferred_element_type=F32
            ) * (1.0 / math.sqrt(HEAD_DIM))
            masked = jnp.where(allowed, scores, -jnp.inf)
            weights = jnp.exp(masked - jnp.max(masked, axis=-1, keepdims=True))
            probs = (weights / jnp.sum(weights, axis=-1, keepdims=True)).astype(BF16)
            attended = jnp.dot(probs, values, preferred_element_type=F32)
            resid[:, cols] = (res_ref[:, cols].astype(F32) + attended).astype(BF16)

    def peers(body):
        for other in range(nh):
            @pl.when(other != h)
            def _(other=other):
                body(other)

    def exchange(buf, send, recv):
        peers(lambda o: remote(buf.at[h], buf.at[h], send.at[o], recv.at[h], c, o).start())
        peers(lambda o: remote(buf.at[o], buf.at[o], send.at[o], recv.at[o], c, o).wait_recv())
        total = buf[0]
        for other in range(1, nh):
            total = total + buf[other]
        return total

    def exchange_end(buf, send, recv):
        peers(lambda o: remote(buf.at[h], buf.at[h], send.at[o], recv.at[h], c, o).wait_send())

    resid_own = resid[...].astype(F32)
    squares[h] = jnp.broadcast_to(
        jnp.sum(resid_own * resid_own, axis=1, keepdims=True), (rows, TILE)
    )
    rms = jnp.sqrt(exchange(squares, sq_send, sq_recv)[:, :1] / width + 1e-05)

    normed = (resid[...].astype(F32) / rms * gain_ref[...]).astype(BF16)
    for b in range(nb):
        nbuf[b] = normed[:, b * dc : (b + 1) * dc].reshape(nh, sub, dc)

    def hop_one(b, other):
        to_c = h * nb + b
        return remote(
            nbuf.at[b, other], xall.at[c, other], n_send.at[b, other], n_recv.at[c], to_c, other
        )

    for b in range(nb):
        for other in range(nh):
            mine = (h * nb + b == c) & (other == h)

            @pl.when(jnp.logical_not(mine))
            def _(b=b, other=other):
                hop_one(b, other).start()

            @pl.when(mine)
            def _(b=b, other=other):
                xall[c, other] = nbuf[b, other]

    source_h = c // nb
    for other in range(nc):
        @pl.when((other != c) | (source_h != h))
        def _(other=other):
            remote(
                xall.at[other, h], xall.at[other, h], n_send.at[0, 0], n_recv.at[other],
                other, source_h,
            ).wait_recv()

    def hop_two(row_h, to_h):
        return remote(
            xall.at[:, row_h], xall.at[:, row_h], x_send.at[to_h], x_recv.at[row_h], c, to_h
        )

    peers(lambda o: hop_two(h, o).start())
    for copy in weight_copies:
        copy.wait()
    peers(lambda o: hop_two(o, o).wait_recv())

    def cols_of(j):
        return pl.ds(pl.multiple_of(j * cw, cw), cw)

    def rs_copy(j, dest, to_c, buf, recv):
        return remote(
            part.at[j, dest], buf.at[j, dest], rs_send.at[j, dest], recv.at[j, dest], to_c, h
        )

    def go_right(j, dest):
        return rs_copy(j, dest, lax.rem(c + 1, nc), fromleft, right_recv)

    def go_left(j, dest):
        return rs_copy(j, dest, lax.rem(c + nc - 1, nc), fromright, left_recv)

    def multiply(j, carry):
        def block(i, inner_carry):
            x = xall[i].reshape(rows, dc)
            tmp[i, :, 0:cw] = jnp.dot(x, wg[:, cols_of(j)], preferred_element_type=F32)
            tmp[i, :, cw : 2 * cw] = jnp.dot(x, wu[:, cols_of(j)], preferred_element_type=F32)
            part[j, i] = tmp[i].astype(BF16)
            return inner_carry

        lax.fori_loop(0, nc, block, 0)
        own[j] = tmp[c]
        for dest in range(nc - 1, 0, -1):
            @pl.when(c == 0)
            def _(dest=dest):
                go_right(j, dest).start()
        for dest in range(nc - 1):
            @pl.when(c == nc - 1)
            def _(dest=dest):
                go_left(j, dest).start()
        return carry

    lax.fori_loop(0, chunks, multiply, 0)

    def reduce_on(j):
        for far in range(nc - 1):
            dest = nc - 1 - far

            @pl.when((c > 0) & (c < dest))
            def _(dest=dest):
                go_right(j, dest).wait_recv()
                part[j, dest] = (part[j, dest].astype(F32) + fromleft[j, dest].astype(F32)).astype(BF16)
                go_right(j, dest).start()

            @pl.when((c < nc - 1) & (c > far))
            def _(dest=far):
                go_left(j, dest).wait_recv()
                part[j, dest] = (part[j, dest].astype(F32) + fromright[j, dest].astype(F32)).astype(BF16)
                go_left(j, dest).start()

    def gather_copy(j, block, direction):
        to_c = lax.rem(c + 1, nc) if direction == 0 else lax.rem(c + nc - 1, nc)
        return remote(
            gathered.at[j, block], gathered.at[j, block], ag_send.at[direction, j, block],
            ag_recv.at[j, block], to_c, h,
        )

    loss_acc[...] = jnp.zeros_like(loss_acc)

    def features(j):
        @pl.when(c > 0)
        def _():
            go_right(j, c).wait_recv()
            own[j] = own[j] + fromleft[j, c].astype(F32)

        @pl.when(c < nc - 1)
        def _():
            go_left(j, c).wait_recv()
            own[j] = own[j] + fromright[j, c].astype(F32)

        gate = own[j, :, 0:cw]
        up = own[j, :, cw : 2 * cw]
        lifted = jnp.maximum(gate, 0.0)
        squared = lifted * lifted
        act = squared * up
        keep = keep_wide[:, cols_of(j)].astype(F32)
        differ = act - feats_ref[:, cols_of(j)].astype(F32)
        grad_act = keep * differ
        loss_acc[...] += grad_act * differ
        gathered[j, c, :, 0:cw] = act.astype(BF16)
        gathered[j, c, :, cw : 2 * cw] = (grad_act * up * 2.0 * lifted).astype(BF16)
        gathered[j, c, :, 2 * cw : 3 * cw] = (grad_act * squared).astype(BF16)

        @pl.when(c < nc - 1)
        def _():
            gather_copy(j, c, 0).start()

        @pl.when(c > 0)
        def _():
            gather_copy(j, c, 1).start()

    def forward(j):
        for far in range(1, nc):
            @pl.when(c >= far)
            def _(far=far):
                block = lax.rem(c - far + nc, nc)
                gather_copy(j, block, 0).wait_recv()

                @pl.when(c < nc - 1)
                def _():
                    gather_copy(j, block, 0).start()

            @pl.when(c + far < nc)
            def _(far=far):
                block = lax.rem(c + far, nc)
                gather_copy(j, block, 1).wait_recv()

                @pl.when(c > 0)
                def _():
                    gather_copy(j, block, 1).start()

    contract = (((1,), (1,)), ((), ()))
    acc_down[...] = jnp.zeros_like(acc_down)
    acc_grad[...] = jnp.zeros_like(acc_grad)

    def accumulate(j):
        def block(i, carry):
            hidden = gathered[j, i, :, 0:cw]
            grad_gate = gathered[j, i, :, cw : 2 * cw]
            grad_up = gathered[j, i, :, 2 * cw : 3 * cw]
            acc_down[i] += jnp.dot(hidden, wd[cols_of(j), :], preferred_element_type=F32)
            acc_grad[i] += lax.dot_general(
                grad_gate, wg[:, cols_of(j)], contract, preferred_element_type=F32
            ) + lax.dot_general(grad_up, wu[:, cols_of(j)], contract, preferred_element_type=F32)
            return carry

        lax.fori_loop(0, nc, block, 0)

    def step(i, carry):
        @pl.when(i < chunks)
        def _():
            reduce_on(i)

        @pl.when((i >= 1) & (i < chunks + 1))
        def _():
            features(i - 1)

        @pl.when(i >= 2)
        def _():
            forward(i - 2)
            accumulate(i - 2)

        return carry

    lax.fori_loop(0, chunks + 2, step, 0)

    loss_part = jnp.sum(jnp.sum(loss_acc[...], axis=1, keepdims=True), axis=0, keepdims=True)
    count_part = jnp.sum(
        jnp.sum(keep_ref[...].astype(F32), axis=1, keepdims=True), axis=0, keepdims=True
    ) * TILE
    line = lax.broadcasted_iota(jnp.int32, (8, TILE), 0)
    loss_head[h] = jnp.where(line == 0, loss_part, count_part)
    peers(lambda o: remote(loss_head.at[h], loss_head.at[h], lh_send.at[o], lh_recv.at[h], c, o).start())

    for p in range(npair):
        for g in range(nhead):
            o = g * npair + p
            for i in range(nc):
                sums[p, g, i, 0] = acc_down[i, o * sub : (o + 1) * sub].astype(BF16)
                sums[p, g, i, 1] = acc_grad[i, o * sub : (o + 1) * sub].astype(BF16)

    def pair_copy(p):
        return remote(
            sums.at[p], pair_in.at[my_pair], p_send.at[p], p_recv.at[my_pair], c, my_head * npair + p
        )

    def pair_wait(p):
        return remote(
            sums.at[p], pair_in.at[p], p_send.at[p], p_recv.at[p], c, my_head * npair + p
        )

    for p in range(npair):
        @pl.when(p != my_pair)
        def _(p=p):
            pair_copy(p).start()
    for p in range(npair):
        @pl.when(p != my_pair)
        def _(p=p):
            pair_wait(p).wait_recv()

            def add(i, carry):
                g, k = i // nc, i % nc
                sums[my_pair, g, k] = (
                    sums[my_pair, g, k].astype(F32) + pair_in[p, g, k].astype(F32)
                ).astype(BF16)
                return carry

            lax.fori_loop(0, nhead * nc, add, 0)

    def head_copy(g):
        return remote(
            sums.at[my_pair, g], head_in.at[my_head], h_send.at[g], h_recv.at[my_head],
            c, g * npair + my_pair,
        )

    def head_wait(g):
        return remote(
            sums.at[my_pair, g], head_in.at[g], h_send.at[g], h_recv.at[g],
            c, g * npair + my_pair,
        )

    for g in range(nhead):
        @pl.when(g != my_head)
        def _(g=g):
            head_copy(g).start()

    peers(lambda o: remote(loss_head.at[o], loss_head.at[o], lh_send.at[o], lh_recv.at[o], c, o).wait_recv())
    head_total = loss_head[0]
    for other in range(1, nh):
        head_total = head_total + loss_head[other]
    loss_ctx[c] = head_total

    def loss_copy(block, to_c):
        return remote(
            loss_ctx.at[block], loss_ctx.at[block], lc_send.at[to_c], lc_recv.at[block], to_c, h
        )

    for other in range(nc):
        @pl.when(other != c)
        def _(other=other):
            loss_copy(c, other).start()

    for g in range(nhead):
        @pl.when(g != my_head)
        def _(g=g):
            head_wait(g).wait_recv()

            def add(k, carry):
                sums[my_pair, my_head, k] = (
                    sums[my_pair, my_head, k].astype(F32) + head_in[g, k].astype(F32)
                ).astype(BF16)
                return carry

            lax.fori_loop(0, nc, add, 0)

    to_h = c // nb
    slot = lax.rem(c, nb) if nb > 1 else 0

    def final_copy(block):
        return remote(
            sums.at[my_pair, my_head, block], final.at[slot, h], f_send.at[block],
            f_recv.at[slot, h], block, to_h,
        )

    for block in range(nc):
        mine = (block == c) & (to_h == h)

        @pl.when(jnp.logical_not(mine))
        def _(block=block):
            final_copy(block).start()

        @pl.when(mine)
        def _(block=block):
            final[slot, h] = sums[my_pair, my_head, block]

    for b in range(nb):
        for other in range(nh):
            from_c = h * nb + b

            @pl.when((from_c != c) | (other != h))
            def _(b=b, other=other, from_c=from_c):
                remote(
                    final.at[b, other], final.at[b, other], f_send.at[0], f_recv.at[b, other],
                    from_c, other,
                ).wait_recv()

    inner_part = jnp.zeros((rows, 1), F32)
    for b in range(nb):
        cols = slice(b * dc, (b + 1) * dc)
        down = final[b, :, 0].reshape(rows, dc).astype(F32)
        out_ref[:, cols] = (resid[:, cols].astype(F32) + down).astype(BF16)
        grad_norm = final[b, :, 1].reshape(rows, dc).astype(F32)
        inner_part += jnp.sum(
            gain_ref[:, cols] * grad_norm * resid[:, cols].astype(F32), axis=1, keepdims=True
        )
    inner[h] = jnp.broadcast_to(inner_part, (rows, TILE))
    inner_sum = exchange(inner, in_send, in_recv)[:, :1]
    rms = jnp.sqrt(
        functools.reduce(lambda a, b: a + b, [squares[o] for o in range(nh)])[:, :1] / width + 1e-05
    )
    scale = inner_sum / (width * (rms * rms * rms))
    for b in range(nb):
        cols = slice(b * dc, (b + 1) * dc)
        grad_norm = final[b, :, 1].reshape(rows, dc).astype(F32)
        grad_ref[:, cols] = (
            gain_ref[:, cols] * grad_norm / rms - resid[:, cols].astype(F32) * scale
        )

    for other in range(nc):
        @pl.when(other != c)
        def _(other=other):
            loss_copy(other, other).wait_recv()
    total = loss_ctx[0]
    for other in range(1, nc):
        total = total + loss_ctx[other]
    loss_ref[...] = jnp.broadcast_to(total[0:1] / total[1:2], (8, TILE))

    for other in range(nc):
        @pl.when(other > c)
        def _(other=other):
            for copy in kv_copies(c, other):
                copy.wait_send()

        @pl.when(other != c)
        def _(other=other):
            loss_copy(c, other).wait_send()

    exchange_end(squares, sq_send, sq_recv)
    exchange_end(inner, in_send, in_recv)
    for b in range(nb):
        for other in range(nh):
            @pl.when((h * nb + b != c) | (other != h))
            def _(b=b, other=other):
                hop_one(b, other).wait_send()
    peers(lambda o: hop_two(h, o).wait_send())
    peers(lambda o: remote(loss_head.at[h], loss_head.at[h], lh_send.at[o], lh_recv.at[h], c, o).wait_send())

    def drain(j, carry):
        for block in range(nc):
            @pl.when(block > c)
            def _(block=block):
                go_right(j, block).wait_send()

            @pl.when(block < c)
            def _(block=block):
                go_left(j, block).wait_send()

            @pl.when((block <= c) & (c < nc - 1))
            def _(block=block):
                gather_copy(j, block, 0).wait_send()

            @pl.when((block >= c) & (c > 0))
            def _(block=block):
                gather_copy(j, block, 1).wait_send()

        return carry

    lax.fori_loop(0, chunks, drain, 0)
    for p in range(npair):
        @pl.when(p != my_pair)
        def _(p=p):
            pair_copy(p).wait_send()
    for g in range(nhead):
        @pl.when(g != my_head)
        def _(g=g):
            head_copy(g).wait_send()
    for block in range(nc):
        @pl.when((block != c) | (to_h != h))
        def _(block=block):
            final_copy(block).wait_send()


def local(
    student_query, teacher_keys, teacher_values, band_span, residual_in, norm_gain,
    w_gate, w_up, w_down, teacher_feats, keep_tiles,
):
    nc, nhead, npair = (lax.axis_size(a) for a in ("ctx", "head", "pair"))
    nh = nhead * npair
    nb = nc // nh
    rows, own_cols = residual_in.shape
    sub = rows // nh
    dc, ff = w_gate.shape
    chunks = CHUNKS
    cw = ff // chunks
    kv = teacher_keys.shape[1]
    gain = lax.dynamic_slice_in_dim(
        norm_gain, lax.axis_index(("head", "pair")) * own_cols, own_cols, 0
    )
    vmem = pl.BlockSpec(memory_space=pltpu.VMEM)
    hbm = pl.BlockSpec(memory_space=pl.ANY)
    dma = lambda *shape: pltpu.SemaphoreType.DMA(shape)
    kernel = functools.partial(layer_kernel, nc, nhead, npair, chunks)
    layer_out, loss, grad = pl.pallas_call(
        kernel,
        out_shape=(
            jax.ShapeDtypeStruct((rows, own_cols), BF16),
            jax.ShapeDtypeStruct((8, TILE), F32),
            jax.ShapeDtypeStruct((rows, own_cols), F32),
        ),
        in_specs=[vmem] * 6 + [hbm] * 3 + [vmem] * 2,
        out_specs=(vmem, vmem, vmem),
        scratch_shapes=[
            pltpu.VMEM((dc, ff), BF16),
            pltpu.VMEM((dc, ff), BF16),
            pltpu.VMEM((ff, dc), BF16),
            pltpu.VMEM((nc, rows, kv), BF16),
            pltpu.VMEM((nc, rows, kv), BF16),
            pltpu.VMEM((rows, own_cols), BF16),
            pltpu.VMEM((nh, rows, TILE), F32),
            pltpu.VMEM((nb, nh, sub, dc), BF16),
            pltpu.VMEM((nc, nh, sub, dc), BF16),
            pltpu.VMEM((nc, rows, 2 * cw), F32),
            pltpu.VMEM((chunks, nc, rows, 2 * cw), BF16),
            pltpu.VMEM((chunks, nc, rows, 2 * cw), BF16),
            pltpu.VMEM((chunks, nc, rows, 2 * cw), BF16),
            pltpu.VMEM((chunks, rows, 2 * cw), F32),
            pltpu.VMEM((chunks, nc, rows, 3 * cw), BF16),
            pltpu.VMEM((nc, rows, dc), F32),
            pltpu.VMEM((nc, rows, dc), F32),
            pltpu.VMEM((rows, ff), BF16),
            pltpu.VMEM((npair, nhead, nc, 2, sub, dc), BF16),
            pltpu.VMEM((npair, nhead, nc, 2, sub, dc), BF16),
            pltpu.VMEM((nhead, nc, 2, sub, dc), BF16),
            pltpu.VMEM((nb, nh, 2, sub, dc), BF16),
            pltpu.VMEM((nh, rows, TILE), F32),
            pltpu.VMEM((nh, 8, TILE), F32),
            pltpu.VMEM((nc, 8, TILE), F32),
            pltpu.VMEM((rows, cw), F32),
            dma(3),
            dma(2, nc), dma(2, nc),
            dma(nh), dma(nh),
            dma(nb, nh), dma(nc),
            dma(nh), dma(nh),
            dma(chunks, nc), dma(chunks, nc), dma(chunks, nc),
            dma(2, chunks, nc), dma(chunks, nc),
            dma(npair), dma(npair),
            dma(nhead), dma(nhead),
            dma(nc), dma(nb, nh),
            dma(nh), dma(nh),
            dma(nh), dma(nh),
            dma(nc), dma(nc),
        ],
        compiler_params=pltpu.CompilerParams(
            collective_id=0, has_side_effects=True, vmem_limit_bytes=60 * 1024 * 1024
        ),
        cost_estimate=pl.CostEstimate(
            flops=10 * nc * rows * dc * ff, bytes_accessed=6 * dc * ff, transcendentals=0
        ),
    )(
        student_query, teacher_keys, teacher_values, band_span.reshape(rows, 1), residual_in,
        gain.reshape(1, own_cols), w_gate, w_up, w_down, teacher_feats, keep_tiles,
    )
    return (layer_out, loss[0, :1], grad)


def solution(mesh):
    in_specs = (
        P(("groups", "ctx"), ("head", "pair")),
        P(("groups", "ctx"), ("head", "pair")),
        P(("groups", "ctx"), ("head", "pair")),
        P(("groups", "ctx")),
        P(("groups", "ctx"), ("head", "pair")),
        P(),
        P("ctx", ("head", "pair")),
        P("ctx", ("head", "pair")),
        P(("head", "pair"), "ctx"),
        P(("groups", "ctx"), ("head", "pair")),
        P(("groups", "ctx"), ("head", "pair")),
    )
    out_specs = (
        P(("groups", "ctx"), ("head", "pair")),
        P("groups"),
        P(("groups", "ctx"), ("head", "pair")),
    )
    return jax.shard_map(local, mesh=mesh, in_specs=in_specs, out_specs=out_specs, check_vma=False)
```

```python
import functools
import math

import jax
import jax.numpy as jnp
from jax import lax
from jax.experimental import pallas as pl
from jax.experimental.pallas import tpu as pltpu
from jax.sharding import PartitionSpec as P

HEAD_DIM = 128
TILE = 128
CHUNKS = 7
MESH = pl.DeviceIdType.MESH
F32 = jnp.float32
BF16 = jnp.bfloat16


def layer_kernel(
    nc, nhead, npair, chunks,
    q_ref, k_ref, v_ref, span_ref, res_ref, gain_ref, wg_hbm, wu_hbm, wd_hbm, feats_ref, keep_ref,
    out_ref, loss_ref, grad_ref,
    wg, wu, wd, kbuf, vbuf, resid, squares, nbuf, xall, tmp, part, fromleft, fromright, own,
    gathered, acc_down, acc_grad, keep_wide, sums, pair_in, head_in, final, inner, loss_head,
    loss_ctx, loss_acc,
    w_sem, kv_send, kv_recv, sq_send, sq_recv, n_send, n_recv, x_send, x_recv, rs_send, right_recv,
    left_recv, ag_send, ag_recv, p_send, p_recv, h_send, h_recv, f_send, f_recv, in_send, in_recv,
    lh_send, lh_recv, lc_send, lc_recv,
):
    nh = nhead * npair
    nb = nc // nh
    rows = q_ref.shape[0]
    sub = rows // nh
    dc = wg.shape[0]
    width = nc * dc
    ff = wg.shape[1]
    cw = ff // chunks
    c = lax.axis_index("ctx")
    my_head = lax.axis_index("head")
    my_pair = lax.axis_index("pair")
    h = my_head * npair + my_pair

    def remote(src, dst, send, recv, to_c, to_h):
        return pltpu.make_async_remote_copy(
            src_ref=src, dst_ref=dst, send_sem=send, recv_sem=recv,
            device_id={"ctx": to_c, "head": to_h // npair, "pair": to_h % npair},
            device_id_type=MESH,
        )

    weight_copies = [
        pltpu.make_async_copy(a, b, w_sem.at[i])
        for i, (a, b) in enumerate(((wg_hbm, wg), (wu_hbm, wu), (wd_hbm, wd)))
    ]
    for copy in weight_copies:
        copy.start()

    barrier = pltpu.get_barrier_semaphore()

    def greet(i, carry):
        to_c, to_h = i // nh, i % nh

        @pl.when((to_c != c) | (to_h != h))
        def _():
            pl.semaphore_signal(
                barrier, inc=1,
                device_id={"ctx": to_c, "head": to_h // npair, "pair": to_h % npair},
                device_id_type=MESH,
            )

        return carry

    lax.fori_loop(0, nc * nh, greet, 0)
    pl.semaphore_wait(barrier, nc * nh - 1)

    def kv_copies(block, to_c):
        return (
            remote(kbuf.at[block], kbuf.at[block], kv_send.at[0, to_c], kv_recv.at[0, block], to_c, h),
            remote(vbuf.at[block], vbuf.at[block], kv_send.at[1, to_c], kv_recv.at[1, block], to_c, h),
        )

    kbuf[c] = k_ref[...]
    vbuf[c] = v_ref[...]
    for other in range(nc):
        @pl.when(other > c)
        def _(other=other):
            for copy in kv_copies(c, other):
                copy.start()
            kbuf[other] = jnp.zeros_like(k_ref)
            vbuf[other] = jnp.zeros_like(v_ref)
    tile_count = keep_ref.shape[0]
    own_cols = res_ref.shape[1]
    gain_own = gain_ref[:, pl.ds(pl.multiple_of(h * own_cols, TILE), own_cols)]
    for t in range(tile_count):
        keep_wide[:, t * TILE : (t + 1) * TILE] = jnp.transpose(
            jnp.broadcast_to(keep_ref[t : t + 1, :].astype(F32), (TILE, rows))
        ).astype(BF16)
    for other in range(nc):
        @pl.when(other < c)
        def _(other=other):
            for copy in kv_copies(other, c):
                copy.wait_recv()

    span_of = jnp.transpose(jnp.broadcast_to(span_ref[...].astype(F32), (TILE, rows)))[:, :1]
    span_of = span_of.astype(jnp.int32)
    span = nc * rows
    key_pos = lax.broadcasted_iota(jnp.int32, (rows, span), 1)
    query_pos = c * rows + lax.broadcasted_iota(jnp.int32, (rows, span), 0)
    distance = query_pos - key_pos
    allowed = (distance >= 0) & (distance < span_of)
    kv_heads = k_ref.shape[1] // HEAD_DIM
    heads = q_ref.shape[1] // HEAD_DIM
    per = heads // kv_heads
    for kv in range(kv_heads):
        kcols = slice(kv * HEAD_DIM, (kv + 1) * HEAD_DIM)
        keys = kbuf[:, :, kcols].reshape(span, HEAD_DIM)
        values = vbuf[:, :, kcols].reshape(span, HEAD_DIM)
        for a in range(kv * per, (kv + 1) * per):
            cols = slice(a * HEAD_DIM, (a + 1) * HEAD_DIM)
            scores = lax.dot_general(
                q_ref[:, cols], keys, (((1,), (1,)), ((), ())), preferred_element_type=F32
            ) * (1.0 / math.sqrt(HEAD_DIM))
            masked = jnp.where(allowed, scores, -jnp.inf)
            weights = jnp.exp(masked - jnp.max(masked, axis=-1, keepdims=True))
            probs = (weights / jnp.sum(weights, axis=-1, keepdims=True)).astype(BF16)
            attended = jnp.dot(probs, values, preferred_element_type=F32)
            resid[:, cols] = (res_ref[:, cols].astype(F32) + attended).astype(BF16)

    def peers(body):
        for other in range(nh):
            @pl.when(other != h)
            def _(other=other):
                body(other)

    def exchange(buf, send, recv):
        peers(lambda o: remote(buf.at[h], buf.at[h], send.at[o], recv.at[h], c, o).start())
        peers(lambda o: remote(buf.at[o], buf.at[o], send.at[o], recv.at[o], c, o).wait_recv())
        total = buf[0]
        for other in range(1, nh):
            total = total + buf[other]
        return total

    def exchange_end(buf, send, recv):
        peers(lambda o: remote(buf.at[h], buf.at[h], send.at[o], recv.at[h], c, o).wait_send())

    resid_own = resid[...].astype(F32)
    squares[h] = jnp.broadcast_to(
        jnp.sum(resid_own * resid_own, axis=1, keepdims=True), (rows, TILE)
    )
    rms = jnp.sqrt(exchange(squares, sq_send, sq_recv)[:, :1] / width + 1e-05)

    normed = (resid[...].astype(F32) / rms * gain_own).astype(BF16)
    for b in range(nb):
        nbuf[b] = normed[:, b * dc : (b + 1) * dc].reshape(nh, sub, dc)

    def hop_one(b, other):
        to_c = h * nb + b
        return remote(
            nbuf.at[b, other], xall.at[c, other], n_send.at[b, other], n_recv.at[c], to_c, other
        )

    for b in range(nb):
        for other in range(nh):
            mine = (h * nb + b == c) & (other == h)

            @pl.when(jnp.logical_not(mine))
            def _(b=b, other=other):
                hop_one(b, other).start()

            @pl.when(mine)
            def _(b=b, other=other):
                xall[c, other] = nbuf[b, other]

    source_h = c // nb
    for other in range(nc):
        @pl.when((other != c) | (source_h != h))
        def _(other=other):
            remote(
                xall.at[other, h], xall.at[other, h], n_send.at[0, 0], n_recv.at[other],
                other, source_h,
            ).wait_recv()

    def hop_two(row_h, to_h):
        return remote(
            xall.at[:, row_h], xall.at[:, row_h], x_send.at[to_h], x_recv.at[row_h], c, to_h
        )

    peers(lambda o: hop_two(h, o).start())
    for copy in weight_copies:
        copy.wait()
    peers(lambda o: hop_two(o, o).wait_recv())

    def cols_of(j):
        return pl.ds(pl.multiple_of(j * cw, cw), cw)

    def rs_copy(j, dest, to_c, buf, recv):
        return remote(
            part.at[j, dest], buf.at[j, dest], rs_send.at[j, dest], recv.at[j, dest], to_c, h
        )

    def go_right(j, dest):
        return rs_copy(j, dest, lax.rem(c + 1, nc), fromleft, right_recv)

    def go_left(j, dest):
        return rs_copy(j, dest, lax.rem(c + nc - 1, nc), fromright, left_recv)

    group = min(nc, 4)

    def multiply(j):
        def block(i, carry):
            at = pl.ds(i * group, group)
            x = xall[at].reshape(group * rows, dc)
            for k, w in enumerate((wg, wu)):
                cols = slice(k * cw, (k + 1) * cw)
                y = jnp.dot(x, w[:, cols_of(j)], preferred_element_type=F32)
                tmp[at, :, cols] = y.reshape(group, rows, cw)
                part[j, at, :, cols] = y.astype(BF16).reshape(group, rows, cw)
            return carry

        lax.fori_loop(0, nc // group, block, 0)
        own[j] = tmp[c]
        for far in range(nc - 1):
            @pl.when(c == 0)
            def _(far=far):
                go_right(j, nc - 1 - far).start()

            @pl.when(c == nc - 1)
            def _(far=far):
                go_left(j, far).start()

    def reduce_right(j):
        for far in range(nc - 2):
            dest = nc - 1 - far

            @pl.when(c < dest)
            def _(dest=dest):
                go_right(j, dest).wait_recv()
                part[j, dest] = (part[j, dest].astype(F32) + fromleft[j, dest].astype(F32)).astype(BF16)
                go_right(j, dest).start()

    def reduce_left(j):
        for dest in range(nc - 2):
            @pl.when(c > dest)
            def _(dest=dest):
                go_left(j, dest).wait_recv()
                part[j, dest] = (part[j, dest].astype(F32) + fromright[j, dest].astype(F32)).astype(BF16)
                go_left(j, dest).start()

    def gather_copy(j, block, direction):
        to_c = lax.rem(c + 1, nc) if direction == 0 else lax.rem(c + nc - 1, nc)
        return remote(
            gathered.at[j, block], gathered.at[j, block], ag_send.at[direction, j, block],
            ag_recv.at[j, block], to_c, h,
        )

    loss_acc[...] = jnp.zeros_like(loss_acc)

    def features(j):
        @pl.when(c > 0)
        def _():
            go_right(j, c).wait_recv()
            own[j] = own[j] + fromleft[j, c].astype(F32)

        @pl.when(c < nc - 1)
        def _():
            go_left(j, c).wait_recv()
            own[j] = own[j] + fromright[j, c].astype(F32)

        gate = own[j, :, 0:cw]
        up = own[j, :, cw : 2 * cw]
        lifted = jnp.maximum(gate, 0.0)
        squared = lifted * lifted
        act = squared * up
        keep = keep_wide[:, cols_of(j)].astype(F32)
        differ = act - feats_ref[:, cols_of(j)].astype(F32)
        grad_act = keep * differ
        loss_acc[...] += grad_act * differ
        gathered[j, c, :, 0:cw] = act.astype(BF16)
        gathered[j, c, :, cw : 2 * cw] = (grad_act * up * 2.0 * lifted).astype(BF16)
        gathered[j, c, :, 2 * cw : 3 * cw] = (grad_act * squared).astype(BF16)

        @pl.when(c < nc - 1)
        def _():
            gather_copy(j, c, 0).start()

        @pl.when(c > 0)
        def _():
            gather_copy(j, c, 1).start()

    def forward(j, far):
        @pl.when(c >= far)
        def _():
            block = lax.rem(c - far + nc, nc)
            gather_copy(j, block, 0).wait_recv()

            @pl.when(c < nc - 1)
            def _():
                gather_copy(j, block, 0).start()

        @pl.when(c + far < nc)
        def _():
            block = lax.rem(c + far, nc)
            gather_copy(j, block, 1).wait_recv()

            @pl.when(c > 0)
            def _():
                gather_copy(j, block, 1).start()

    contract = (((1,), (1,)), ((), ()))
    acc_down[...] = jnp.zeros_like(acc_down)
    acc_grad[...] = jnp.zeros_like(acc_grad)

    def accumulate(j):
        def block(i, carry):
            at = pl.ds(i * group, group)

            def rows_of(k):
                return gathered[j, at, :, k * cw : (k + 1) * cw].reshape(group * rows, cw)

            down = jnp.dot(rows_of(0), wd[cols_of(j), :], preferred_element_type=F32)
            acc_down[at] += down.reshape(group, rows, dc)
            grad = lax.dot_general(
                rows_of(1), wg[:, cols_of(j)], contract, preferred_element_type=F32
            ) + lax.dot_general(rows_of(2), wu[:, cols_of(j)], contract, preferred_element_type=F32)
            acc_grad[at] += grad.reshape(group, rows, dc)
            return carry

        lax.fori_loop(0, nc // group, block, 0)

    ahead = 2
    feature_lag = max(nc - 2, 1)
    inside = (c > 0) & (c < nc - 1)

    def step(i, carry):
        def when(lag, body, also=True):
            j = i - lag

            @pl.when((j >= 0) & (j < chunks) & also)
            def _():
                body(j)

        when(-ahead, multiply)
        when(c - 1, reduce_right, inside)
        when(nc - 2 - c, reduce_left, inside)
        when(feature_lag, features)
        for far in range(1, nc):
            when(feature_lag + far, functools.partial(forward, far=far))
        when(feature_lag + nc - 1, accumulate)
        return carry

    for j in range(ahead):
        multiply(j)
    lax.fori_loop(0, chunks + feature_lag + nc - 1, step, 0)

    loss_part = jnp.sum(jnp.sum(loss_acc[...], axis=1, keepdims=True), axis=0, keepdims=True)
    count_part = jnp.sum(
        jnp.sum(keep_ref[...].astype(F32), axis=1, keepdims=True), axis=0, keepdims=True
    ) * TILE
    line = lax.broadcasted_iota(jnp.int32, (8, TILE), 0)
    loss_head[h] = jnp.where(line == 0, loss_part, count_part)
    peers(lambda o: remote(loss_head.at[h], loss_head.at[h], lh_send.at[o], lh_recv.at[h], c, o).start())

    for p in range(npair):
        for g in range(nhead):
            o = g * npair + p
            for i in range(nc):
                sums[p, g, i, 0] = acc_down[i, o * sub : (o + 1) * sub].astype(BF16)
                sums[p, g, i, 1] = acc_grad[i, o * sub : (o + 1) * sub].astype(BF16)

    def pair_copy(p):
        return remote(
            sums.at[p], pair_in.at[my_pair], p_send.at[p], p_recv.at[my_pair], c, my_head * npair + p
        )

    def pair_wait(p):
        return remote(
            sums.at[p], pair_in.at[p], p_send.at[p], p_recv.at[p], c, my_head * npair + p
        )

    for p in range(npair):
        @pl.when(p != my_pair)
        def _(p=p):
            pair_copy(p).start()
    for p in range(npair):
        @pl.when(p != my_pair)
        def _(p=p):
            pair_wait(p).wait_recv()

            def add(i, carry):
                g, k = i // nc, i % nc
                sums[my_pair, g, k] = (
                    sums[my_pair, g, k].astype(F32) + pair_in[p, g, k].astype(F32)
                ).astype(BF16)
                return carry

            lax.fori_loop(0, nhead * nc, add, 0)

    def head_copy(g):
        return remote(
            sums.at[my_pair, g], head_in.at[my_head], h_send.at[g], h_recv.at[my_head],
            c, g * npair + my_pair,
        )

    def head_wait(g):
        return remote(
            sums.at[my_pair, g], head_in.at[g], h_send.at[g], h_recv.at[g],
            c, g * npair + my_pair,
        )

    for g in range(nhead):
        @pl.when(g != my_head)
        def _(g=g):
            head_copy(g).start()

    peers(lambda o: remote(loss_head.at[o], loss_head.at[o], lh_send.at[o], lh_recv.at[o], c, o).wait_recv())
    head_total = loss_head[0]
    for other in range(1, nh):
        head_total = head_total + loss_head[other]
    loss_ctx[c] = head_total

    def loss_copy(block, to_c):
        return remote(
            loss_ctx.at[block], loss_ctx.at[block], lc_send.at[to_c], lc_recv.at[block], to_c, h
        )

    for other in range(nc):
        @pl.when(other != c)
        def _(other=other):
            loss_copy(c, other).start()

    for g in range(nhead):
        @pl.when(g != my_head)
        def _(g=g):
            head_wait(g).wait_recv()

            def add(k, carry):
                sums[my_pair, my_head, k] = (
                    sums[my_pair, my_head, k].astype(F32) + head_in[g, k].astype(F32)
                ).astype(BF16)
                return carry

            lax.fori_loop(0, nc, add, 0)

    to_h = c // nb
    slot = lax.rem(c, nb) if nb > 1 else 0

    def final_copy(block):
        return remote(
            sums.at[my_pair, my_head, block], final.at[slot, h], f_send.at[block],
            f_recv.at[slot, h], block, to_h,
        )

    for block in range(nc):
        mine = (block == c) & (to_h == h)

        @pl.when(jnp.logical_not(mine))
        def _(block=block):
            final_copy(block).start()

        @pl.when(mine)
        def _(block=block):
            final[slot, h] = sums[my_pair, my_head, block]

    for b in range(nb):
        for other in range(nh):
            from_c = h * nb + b

            @pl.when((from_c != c) | (other != h))
            def _(b=b, other=other, from_c=from_c):
                remote(
                    final.at[b, other], final.at[b, other], f_send.at[0], f_recv.at[b, other],
                    from_c, other,
                ).wait_recv()

    inner_part = jnp.zeros((rows, 1), F32)
    for b in range(nb):
        cols = slice(b * dc, (b + 1) * dc)
        down = final[b, :, 0].reshape(rows, dc).astype(F32)
        out_ref[:, cols] = (resid[:, cols].astype(F32) + down).astype(BF16)
        grad_norm = final[b, :, 1].reshape(rows, dc).astype(F32)
        inner_part += jnp.sum(
            gain_own[:, cols] * grad_norm * resid[:, cols].astype(F32), axis=1, keepdims=True
        )
    inner[h] = jnp.broadcast_to(inner_part, (rows, TILE))
    inner_sum = exchange(inner, in_send, in_recv)[:, :1]
    rms = jnp.sqrt(
        functools.reduce(lambda a, b: a + b, [squares[o] for o in range(nh)])[:, :1] / width + 1e-05
    )
    scale = inner_sum / (width * (rms * rms * rms))
    for b in range(nb):
        cols = slice(b * dc, (b + 1) * dc)
        grad_norm = final[b, :, 1].reshape(rows, dc).astype(F32)
        grad_ref[:, cols] = (
            gain_own[:, cols] * grad_norm / rms - resid[:, cols].astype(F32) * scale
        )

    for other in range(nc):
        @pl.when(other != c)
        def _(other=other):
            loss_copy(other, other).wait_recv()
    total = loss_ctx[0]
    for other in range(1, nc):
        total = total + loss_ctx[other]
    loss_ref[...] = total[0:1, 0:1] / total[1:2, 0:1]

    for other in range(nc):
        @pl.when(other > c)
        def _(other=other):
            for copy in kv_copies(c, other):
                copy.wait_send()

        @pl.when(other != c)
        def _(other=other):
            loss_copy(c, other).wait_send()

    exchange_end(squares, sq_send, sq_recv)
    exchange_end(inner, in_send, in_recv)
    for b in range(nb):
        for other in range(nh):
            @pl.when((h * nb + b != c) | (other != h))
            def _(b=b, other=other):
                hop_one(b, other).wait_send()
    peers(lambda o: hop_two(h, o).wait_send())
    peers(lambda o: remote(loss_head.at[h], loss_head.at[h], lh_send.at[o], lh_recv.at[h], c, o).wait_send())

    def drain(j, carry):
        for block in range(nc):
            @pl.when(block > c)
            def _(block=block):
                go_right(j, block).wait_send()

            @pl.when(block < c)
            def _(block=block):
                go_left(j, block).wait_send()

            @pl.when((block <= c) & (c < nc - 1))
            def _(block=block):
                gather_copy(j, block, 0).wait_send()

            @pl.when((block >= c) & (c > 0))
            def _(block=block):
                gather_copy(j, block, 1).wait_send()

        return carry

    lax.fori_loop(0, chunks, drain, 0)
    for p in range(npair):
        @pl.when(p != my_pair)
        def _(p=p):
            pair_copy(p).wait_send()
    for g in range(nhead):
        @pl.when(g != my_head)
        def _(g=g):
            head_copy(g).wait_send()
    for block in range(nc):
        @pl.when((block != c) | (to_h != h))
        def _(block=block):
            final_copy(block).wait_send()


def local(
    student_query, teacher_keys, teacher_values, band_span, residual_in, norm_gain,
    w_gate, w_up, w_down, teacher_feats, keep_tiles,
):
    nc, nhead, npair = (lax.axis_size(a) for a in ("ctx", "head", "pair"))
    nh = nhead * npair
    nb = nc // nh
    rows, own_cols = residual_in.shape
    sub = rows // nh
    dc, ff = w_gate.shape
    chunks = CHUNKS
    cw = ff // chunks
    kv = teacher_keys.shape[1]
    vmem = pl.BlockSpec(memory_space=pltpu.VMEM)
    hbm = pl.BlockSpec(memory_space=pl.ANY)
    dma = lambda *shape: pltpu.SemaphoreType.DMA(shape)
    kernel = functools.partial(layer_kernel, nc, nhead, npair, chunks)
    layer_out, loss, grad = pl.pallas_call(
        kernel,
        out_shape=(
            jax.ShapeDtypeStruct((rows, own_cols), BF16),
            jax.ShapeDtypeStruct((1, 1), F32),
            jax.ShapeDtypeStruct((rows, own_cols), F32),
        ),
        in_specs=[vmem] * 6 + [hbm] * 3 + [vmem] * 2,
        out_specs=(vmem, vmem, vmem),
        scratch_shapes=[
            pltpu.VMEM((dc, ff), BF16),
            pltpu.VMEM((dc, ff), BF16),
            pltpu.VMEM((ff, dc), BF16),
            pltpu.VMEM((nc, rows, kv), BF16),
            pltpu.VMEM((nc, rows, kv), BF16),
            pltpu.VMEM((rows, own_cols), BF16),
            pltpu.VMEM((nh, rows, TILE), F32),
            pltpu.VMEM((nb, nh, sub, dc), BF16),
            pltpu.VMEM((nc, nh, sub, dc), BF16),
            pltpu.VMEM((nc, rows, 2 * cw), F32),
            pltpu.VMEM((chunks, nc, rows, 2 * cw), BF16),
            pltpu.VMEM((chunks, nc, rows, 2 * cw), BF16),
            pltpu.VMEM((chunks, nc, rows, 2 * cw), BF16),
            pltpu.VMEM((chunks, rows, 2 * cw), F32),
            pltpu.VMEM((chunks, nc, rows, 3 * cw), BF16),
            pltpu.VMEM((nc, rows, dc), F32),
            pltpu.VMEM((nc, rows, dc), F32),
            pltpu.VMEM((rows, ff), BF16),
            pltpu.VMEM((npair, nhead, nc, 2, sub, dc), BF16),
            pltpu.VMEM((npair, nhead, nc, 2, sub, dc), BF16),
            pltpu.VMEM((nhead, nc, 2, sub, dc), BF16),
            pltpu.VMEM((nb, nh, 2, sub, dc), BF16),
            pltpu.VMEM((nh, rows, TILE), F32),
            pltpu.VMEM((nh, 8, TILE), F32),
            pltpu.VMEM((nc, 8, TILE), F32),
            pltpu.VMEM((rows, cw), F32),
            dma(3),
            dma(2, nc), dma(2, nc),
            dma(nh), dma(nh),
            dma(nb, nh), dma(nc),
            dma(nh), dma(nh),
            dma(chunks, nc), dma(chunks, nc), dma(chunks, nc),
            dma(2, chunks, nc), dma(chunks, nc),
            dma(npair), dma(npair),
            dma(nhead), dma(nhead),
            dma(nc), dma(nb, nh),
            dma(nh), dma(nh),
            dma(nh), dma(nh),
            dma(nc), dma(nc),
        ],
        compiler_params=pltpu.CompilerParams(
            collective_id=0, has_side_effects=True, vmem_limit_bytes=60 * 1024 * 1024
        ),
        cost_estimate=pl.CostEstimate(
            flops=10 * nc * rows * dc * ff, bytes_accessed=6 * dc * ff, transcendentals=0
        ),
    )(
        student_query, teacher_keys, teacher_values, band_span.reshape(1, rows), residual_in,
        norm_gain.reshape(1, -1), w_gate, w_up, w_down, teacher_feats, keep_tiles.T,
    )
    return (layer_out, loss.reshape(1), grad)


def solution(mesh):
    in_specs = (
        P(("groups", "ctx"), ("head", "pair")),
        P(("groups", "ctx"), ("head", "pair")),
        P(("groups", "ctx"), ("head", "pair")),
        P(("groups", "ctx")),
        P(("groups", "ctx"), ("head", "pair")),
        P(),
        P("ctx", ("head", "pair")),
        P("ctx", ("head", "pair")),
        P(("head", "pair"), "ctx"),
        P(("groups", "ctx"), ("head", "pair")),
        P(("groups", "ctx"), ("head", "pair")),
    )
    out_specs = (
        P(("groups", "ctx"), ("head", "pair")),
        P("groups"),
        P(("groups", "ctx"), ("head", "pair")),
    )
    return jax.shard_map(local, mesh=mesh, in_specs=in_specs, out_specs=out_specs, check_vma=False)
```

```python
import functools
import math

import jax
import jax.numpy as jnp
from jax import lax
from jax.experimental import pallas as pl
from jax.experimental.pallas import tpu as pltpu
from jax.sharding import PartitionSpec as P

HEAD_DIM = 128
TILE = 128
CHUNKS = 7
MESH = pl.DeviceIdType.MESH
F32 = jnp.float32
BF16 = jnp.bfloat16


def layer_kernel(
    nc, nhead, npair, chunks,
    q_ref, k_ref, v_ref, span_ref, res_ref, gain_ref, wg_hbm, wu_hbm, wd_hbm, feats_ref, keep_ref,
    out_ref, loss_ref, grad_ref,
    wg, wu, wd, kbuf, vbuf, resid, squares, nbuf, xall, tmp, part, fromleft, fromright, own,
    gathered, acc_down, acc_grad, feats, keeps, terms, sums, pair_in, head_in, final, inner, loss_head,
    loss_ctx, loss_acc,
    w_sem, kv_send, kv_recv, sq_send, sq_recv, n_send, n_recv, x_send, m_send, x_recv, ft_send, ft_recv, kp_send, kp_recv, rs_send, right_recv,
    left_recv, ag_send, ag_recv, p_send, p_recv, h_send, h_recv, f_send, f_recv, in_send, in_recv,
    lh_send, lh_recv, lc_send, lc_recv,
):
    nh = nhead * npair
    nb = nc // nh
    rows = q_ref.shape[0]
    sub = rows // nh
    dc = wg.shape[0]
    width = nc * dc
    ff = wg.shape[1]
    cw = ff // chunks
    c = lax.axis_index("ctx")
    my_head = lax.axis_index("head")
    my_pair = lax.axis_index("pair")
    h = my_head * npair + my_pair

    def remote(src, dst, send, recv, to_c, to_h):
        return pltpu.make_async_remote_copy(
            src_ref=src, dst_ref=dst, send_sem=send, recv_sem=recv,
            device_id={"ctx": to_c, "head": to_h // npair, "pair": to_h % npair},
            device_id_type=MESH,
        )

    weight_copies = [
        pltpu.make_async_copy(a, b, w_sem.at[i])
        for i, (a, b) in enumerate(((wg_hbm, wg), (wu_hbm, wu), (wd_hbm, wd)))
    ]
    for copy in weight_copies:
        copy.start()

    barrier = pltpu.get_barrier_semaphore()

    def greet(i, carry):
        to_c, to_h = i // nh, i % nh

        @pl.when((to_c != c) | (to_h != h))
        def _():
            pl.semaphore_signal(
                barrier, inc=1,
                device_id={"ctx": to_c, "head": to_h // npair, "pair": to_h % npair},
                device_id_type=MESH,
            )

        return carry

    lax.fori_loop(0, nc * nh, greet, 0)
    pl.semaphore_wait(barrier, nc * nh - 1)

    def kv_copies(block, to_c):
        return (
            remote(kbuf.at[block], kbuf.at[block], kv_send.at[0, to_c], kv_recv.at[0, block], to_c, h),
            remote(vbuf.at[block], vbuf.at[block], kv_send.at[1, to_c], kv_recv.at[1, block], to_c, h),
        )

    kbuf[c] = k_ref[...]
    vbuf[c] = v_ref[...]
    for other in range(nc):
        @pl.when(other > c)
        def _(other=other):
            for copy in kv_copies(c, other):
                copy.start()
            kbuf[other] = jnp.zeros_like(k_ref)
            vbuf[other] = jnp.zeros_like(v_ref)
    own_cols = res_ref.shape[1]
    gain_own = gain_ref[:, pl.ds(pl.multiple_of(h * own_cols, TILE), own_cols)]
    keeps[c] = keep_ref[...]

    def keep_copy(block, to_c):
        return remote(keeps.at[block], keeps.at[block], kp_send.at[to_c], kp_recv.at[block], to_c, h)

    for other in range(nc):
        @pl.when(other != c)
        def _(other=other):
            keep_copy(c, other).start()
    feats[c] = feats_ref[...]

    def feats_copy(block, direction):
        to_c = lax.rem(c + 1, nc) if direction == 0 else lax.rem(c + nc - 1, nc)
        return remote(
            feats.at[block], feats.at[block], ft_send.at[direction, block], ft_recv.at[block], to_c, h
        )

    def feats_forward(far):
        @pl.when(c >= far)
        def _():
            block = lax.rem(c - far + nc, nc)
            feats_copy(block, 0).wait_recv()

            @pl.when(c < nc - 1)
            def _():
                feats_copy(block, 0).start()

        @pl.when(c + far < nc)
        def _():
            block = lax.rem(c + far, nc)
            feats_copy(block, 1).wait_recv()

            @pl.when(c > 0)
            def _():
                feats_copy(block, 1).start()

    for other in range(nc):
        @pl.when(other < c)
        def _(other=other):
            for copy in kv_copies(other, c):
                copy.wait_recv()

    @pl.when(c < nc - 1)
    def _():
        feats_copy(c, 0).start()

    @pl.when(c > 0)
    def _():
        feats_copy(c, 1).start()

    span_of = jnp.transpose(jnp.broadcast_to(span_ref[...].astype(F32), (TILE, rows)))[:, :1]
    span_of = span_of.astype(jnp.int32)
    span = nc * rows
    key_pos = lax.broadcasted_iota(jnp.int32, (rows, span), 1)
    query_pos = c * rows + lax.broadcasted_iota(jnp.int32, (rows, span), 0)
    distance = query_pos - key_pos
    allowed = (distance >= 0) & (distance < span_of)
    kv_heads = k_ref.shape[1] // HEAD_DIM
    heads = q_ref.shape[1] // HEAD_DIM
    per = heads // kv_heads
    for kv in range(kv_heads):
        kcols = slice(kv * HEAD_DIM, (kv + 1) * HEAD_DIM)
        keys = kbuf[:, :, kcols].reshape(span, HEAD_DIM)
        values = vbuf[:, :, kcols].reshape(span, HEAD_DIM)
        for a in range(kv * per, (kv + 1) * per):
            cols = slice(a * HEAD_DIM, (a + 1) * HEAD_DIM)
            scores = lax.dot_general(
                q_ref[:, cols], keys, (((1,), (1,)), ((), ())), preferred_element_type=F32
            ) * (1.0 / math.sqrt(HEAD_DIM))
            masked = jnp.where(allowed, scores, -jnp.inf)
            weights = jnp.exp(masked - jnp.max(masked, axis=-1, keepdims=True))
            probs = (weights / jnp.sum(weights, axis=-1, keepdims=True)).astype(BF16)
            attended = jnp.dot(probs, values, preferred_element_type=F32)
            resid[:, cols] = (res_ref[:, cols].astype(F32) + attended).astype(BF16)

    def peers(body):
        for other in range(nh):
            @pl.when(other != h)
            def _(other=other):
                body(other)

    def exchange(buf, send, recv):
        peers(lambda o: remote(buf.at[h], buf.at[h], send.at[o], recv.at[h], c, o).start())
        peers(lambda o: remote(buf.at[o], buf.at[o], send.at[o], recv.at[o], c, o).wait_recv())
        total = buf[0]
        for other in range(1, nh):
            total = total + buf[other]
        return total

    def exchange_end(buf, send, recv):
        peers(lambda o: remote(buf.at[h], buf.at[h], send.at[o], recv.at[h], c, o).wait_send())

    resid_own = resid[...].astype(F32)
    squares[h] = jnp.broadcast_to(
        jnp.sum(resid_own * resid_own, axis=1, keepdims=True), (rows, TILE)
    )
    rms = jnp.sqrt(exchange(squares, sq_send, sq_recv)[:, :1] / width + 1e-05)

    normed = (resid[...].astype(F32) / rms * gain_own).astype(BF16)
    for b in range(nb):
        nbuf[b] = normed[:, b * dc : (b + 1) * dc].reshape(nh, sub, dc)

    def hop_one(b, other):
        to_c = h * nb + b
        return remote(
            nbuf.at[b, other], xall.at[c, other], n_send.at[b, other], n_recv.at[c], to_c, other
        )

    for b in range(nb):
        for other in range(nh):
            mine = (h * nb + b == c) & (other == h)

            @pl.when(jnp.logical_not(mine))
            def _(b=b, other=other):
                hop_one(b, other).start()

            @pl.when(mine)
            def _(b=b, other=other):
                xall[c, other] = nbuf[b, other]

    source_h = c // nb

    def to_head(block, row_h, g):
        return remote(
            xall.at[block, row_h], xall.at[block, row_h], x_send.at[g, block],
            x_recv.at[row_h, block], c, g * npair + my_pair,
        )

    def to_mate(block, row_h, p):
        return remote(
            xall.at[block, row_h], xall.at[block, row_h], m_send.at[p, row_h, block],
            x_recv.at[row_h, block], c, my_head * npair + p,
        )

    def others(count, mine, body):
        for o in range(count):
            @pl.when(o != mine)
            def _(o=o):
                body(o)

    for k in range(nc):
        block = lax.rem(c + k, nc)

        @pl.when((block != c) | (source_h != h))
        def _(block=block):
            remote(
                xall.at[block, h], xall.at[block, h], n_send.at[0, 0], n_recv.at[block],
                block, source_h,
            ).wait_recv()

        others(nhead, my_head, lambda g: to_head(block, h, g).start())
        others(npair, my_pair, lambda p: to_mate(block, h, p).start())
    feats_forward(1)
    for k in range(nc):
        block = lax.rem(c + k, nc)

        def pass_on(g):
            row_h = g * npair + my_pair
            to_head(block, row_h, g).wait_recv()
            others(npair, my_pair, lambda p: to_mate(block, row_h, p).start())

        others(nhead, my_head, pass_on)
    for copy in weight_copies:
        copy.wait()
    for k in range(nc):
        for g in range(nhead):
            others(
                npair, my_pair, lambda p: to_mate(k, g * npair + p, p).wait_recv()
            )
    others(nc, c, lambda o: keep_copy(o, o).wait_recv())

    def cols_of(j):
        return pl.ds(pl.multiple_of(j * cw, cw), cw)

    def rs_copy(j, dest, to_c, buf, recv):
        return remote(
            part.at[j, dest], buf.at[j, dest], rs_send.at[j, dest], recv.at[j, dest], to_c, h
        )

    def go_right(j, dest):
        return rs_copy(j, dest, lax.rem(c + 1, nc), fromleft, right_recv)

    def go_left(j, dest):
        return rs_copy(j, dest, lax.rem(c + nc - 1, nc), fromright, left_recv)

    group = min(nc, 4)

    def multiply(j):
        def block(i, carry):
            at = pl.ds(i * group, group)
            x = xall[at].reshape(group * rows, dc)
            for k, w in enumerate((wg, wu)):
                cols = slice(k * cw, (k + 1) * cw)
                y = jnp.dot(x, w[:, cols_of(j)], preferred_element_type=F32)
                tmp[at, :, cols] = y.reshape(group, rows, cw)
                part[j, at, :, cols] = y.astype(BF16).reshape(group, rows, cw)
            return carry

        lax.fori_loop(0, nc // group, block, 0)
        own[j] = tmp[c]
        for far in range(nc - 1):
            @pl.when(c == 0)
            def _(far=far):
                go_right(j, nc - 1 - far).start()

            @pl.when(c == nc - 1)
            def _(far=far):
                go_left(j, far).start()

    def reduce_right(j):
        for far in range(nc - 2):
            dest = nc - 1 - far

            @pl.when(c < dest)
            def _(dest=dest):
                go_right(j, dest).wait_recv()
                part[j, dest] = (part[j, dest].astype(F32) + fromleft[j, dest].astype(F32)).astype(BF16)
                go_right(j, dest).start()

    def reduce_left(j):
        for dest in range(nc - 2):
            @pl.when(c > dest)
            def _(dest=dest):
                go_left(j, dest).wait_recv()
                part[j, dest] = (part[j, dest].astype(F32) + fromright[j, dest].astype(F32)).astype(BF16)
                go_left(j, dest).start()

    def gather_copy(j, block, direction):
        to_c = lax.rem(c + 1, nc) if direction == 0 else lax.rem(c + nc - 1, nc)
        return remote(
            gathered.at[j, block], gathered.at[j, block], ag_send.at[direction, j, block],
            ag_recv.at[j, block], to_c, h,
        )

    loss_acc[...] = jnp.zeros_like(loss_acc)
    per_chunk = cw // TILE

    def keep_of(j, block):
        wide = [
            jnp.transpose(
                jnp.broadcast_to(
                    keeps[block, pl.ds(j * per_chunk + t, 1), :].astype(F32), (TILE, rows)
                )
            )
            for t in range(per_chunk)
        ]
        return jnp.concatenate(wide, axis=1) if per_chunk > 1 else wide[0]

    def features(j):
        @pl.when(c > 0)
        def _():
            go_right(j, c).wait_recv()
            own[j] = own[j] + fromleft[j, c].astype(F32)

        @pl.when(c < nc - 1)
        def _():
            go_left(j, c).wait_recv()
            own[j] = own[j] + fromright[j, c].astype(F32)

        gate = own[j, :, 0:cw]
        up = own[j, :, cw : 2 * cw]
        lifted = jnp.maximum(gate, 0.0)
        squared = lifted * lifted
        act = squared * up
        differ = act - feats_ref[:, cols_of(j)].astype(F32)
        loss_acc[...] += keep_of(j, c) * differ * differ
        gathered[j, c] = own[j].astype(BF16)

        @pl.when(c < nc - 1)
        def _():
            gather_copy(j, c, 0).start()

        @pl.when(c > 0)
        def _():
            gather_copy(j, c, 1).start()

    def forward(j, far):
        @pl.when(c >= far)
        def _():
            block = lax.rem(c - far + nc, nc)
            gather_copy(j, block, 0).wait_recv()

            @pl.when(c < nc - 1)
            def _():
                gather_copy(j, block, 0).start()

        @pl.when(c + far < nc)
        def _():
            block = lax.rem(c + far, nc)
            gather_copy(j, block, 1).wait_recv()

            @pl.when(c > 0)
            def _():
                gather_copy(j, block, 1).start()

    contract = (((1,), (1,)), ((), ()))
    acc_down[...] = jnp.zeros_like(acc_down)
    acc_grad[...] = jnp.zeros_like(acc_grad)

    def accumulate(j):
        def derive(i, carry):
            gate = gathered[j, i, :, 0:cw].astype(F32)
            up = gathered[j, i, :, cw : 2 * cw].astype(F32)
            lifted = jnp.maximum(gate, 0.0)
            squared = lifted * lifted
            act = squared * up
            differ = act - feats[i, :, cols_of(j)].astype(F32)
            grad_act = keep_of(j, i) * differ
            terms[0, i] = act.astype(BF16)
            terms[1, i] = (grad_act * up * 2.0 * lifted).astype(BF16)
            terms[2, i] = (grad_act * squared).astype(BF16)
            return carry

        lax.fori_loop(0, nc, derive, 0)

        def block(i, carry):
            at = pl.ds(i * group, group)

            def rows_of(k):
                return terms[k, at].reshape(group * rows, cw)

            down = jnp.dot(rows_of(0), wd[cols_of(j), :], preferred_element_type=F32)
            acc_down[at] += down.reshape(group, rows, dc)
            grad = lax.dot_general(
                rows_of(1), wg[:, cols_of(j)], contract, preferred_element_type=F32
            ) + lax.dot_general(rows_of(2), wu[:, cols_of(j)], contract, preferred_element_type=F32)
            acc_grad[at] += grad.reshape(group, rows, dc)
            return carry

        lax.fori_loop(0, nc // group, block, 0)

    ahead = 2
    feature_lag = max(nc - 2, 1)
    inside = (c > 0) & (c < nc - 1)

    def step(i, carry):
        def when(lag, body, also=True):
            j = i - lag

            @pl.when((j >= 0) & (j < chunks) & also)
            def _():
                body(j)

        @pl.when(i < nc - 2)
        def _():
            feats_forward(i + 2)

        when(-ahead, multiply)
        when(c - 1, reduce_right, inside)
        when(nc - 2 - c, reduce_left, inside)
        when(feature_lag, features)
        for far in range(1, nc):
            when(feature_lag + far, functools.partial(forward, far=far))
        when(feature_lag + nc - 1, accumulate)
        return carry

    for j in range(ahead):
        multiply(j)
    lax.fori_loop(0, chunks + feature_lag + nc - 1, step, 0)

    loss_part = jnp.sum(jnp.sum(loss_acc[...], axis=1, keepdims=True), axis=0, keepdims=True)
    count_part = jnp.sum(
        jnp.sum(keep_ref[...].astype(F32), axis=1, keepdims=True), axis=0, keepdims=True
    ) * TILE
    line = lax.broadcasted_iota(jnp.int32, (8, TILE), 0)
    loss_head[h] = jnp.where(line == 0, loss_part, count_part)
    peers(lambda o: remote(loss_head.at[h], loss_head.at[h], lh_send.at[o], lh_recv.at[h], c, o).start())

    def pair_copy(p, k, slot):
        return remote(
            sums.at[p, k], pair_in.at[slot, k], p_send.at[p, k], p_recv.at[slot, k],
            c, my_head * npair + p,
        )

    for k in range(nc):
        for p in range(npair):
            for g in range(nhead):
                o = g * npair + p
                sums[p, k, g, 0] = acc_down[k, o * sub : (o + 1) * sub].astype(BF16)
                sums[p, k, g, 1] = acc_grad[k, o * sub : (o + 1) * sub].astype(BF16)
        others(npair, my_pair, lambda p: pair_copy(p, k, my_pair).start())

    def head_copy(g, k, slot):
        return remote(
            sums.at[my_pair, k, g], head_in.at[slot, k], h_send.at[g, k], h_recv.at[slot, k],
            c, g * npair + my_pair,
        )

    for k in range(nc):
        def add_pair(p):
            pair_copy(p, k, p).wait_recv()
            sums[my_pair, k] = (
                sums[my_pair, k].astype(F32) + pair_in[p, k].astype(F32)
            ).astype(BF16)

        others(npair, my_pair, add_pair)
        others(nhead, my_head, lambda g: head_copy(g, k, my_head).start())

    peers(lambda o: remote(loss_head.at[o], loss_head.at[o], lh_send.at[o], lh_recv.at[o], c, o).wait_recv())
    head_total = loss_head[0]
    for other in range(1, nh):
        head_total = head_total + loss_head[other]
    loss_ctx[c] = head_total

    def loss_copy(block, to_c):
        return remote(
            loss_ctx.at[block], loss_ctx.at[block], lc_send.at[to_c], lc_recv.at[block], to_c, h
        )

    for other in range(nc):
        @pl.when(other != c)
        def _(other=other):
            loss_copy(c, other).start()

    to_h = c // nb
    slot = lax.rem(c, nb) if nb > 1 else 0

    def final_copy(block):
        return remote(
            sums.at[my_pair, block, my_head], final.at[slot, h], f_send.at[block],
            f_recv.at[slot, h], block, to_h,
        )

    for block in range(nc):
        def add_head(g):
            head_copy(g, block, g).wait_recv()
            sums[my_pair, block, my_head] = (
                sums[my_pair, block, my_head].astype(F32) + head_in[g, block].astype(F32)
            ).astype(BF16)

        others(nhead, my_head, add_head)
        mine = (block == c) & (to_h == h)

        @pl.when(jnp.logical_not(mine))
        def _(block=block):
            final_copy(block).start()

        @pl.when(mine)
        def _(block=block):
            final[slot, h] = sums[my_pair, block, my_head]

    for b in range(nb):
        for other in range(nh):
            from_c = h * nb + b

            @pl.when((from_c != c) | (other != h))
            def _(b=b, other=other, from_c=from_c):
                remote(
                    final.at[b, other], final.at[b, other], f_send.at[0], f_recv.at[b, other],
                    from_c, other,
                ).wait_recv()

    inner_part = jnp.zeros((rows, 1), F32)
    for b in range(nb):
        cols = slice(b * dc, (b + 1) * dc)
        down = final[b, :, 0].reshape(rows, dc).astype(F32)
        out_ref[:, cols] = (resid[:, cols].astype(F32) + down).astype(BF16)
        grad_norm = final[b, :, 1].reshape(rows, dc).astype(F32)
        inner_part += jnp.sum(
            gain_own[:, cols] * grad_norm * resid[:, cols].astype(F32), axis=1, keepdims=True
        )
    inner[h] = jnp.broadcast_to(inner_part, (rows, TILE))
    inner_sum = exchange(inner, in_send, in_recv)[:, :1]
    rms = jnp.sqrt(
        functools.reduce(lambda a, b: a + b, [squares[o] for o in range(nh)])[:, :1] / width + 1e-05
    )
    scale = inner_sum / (width * (rms * rms * rms))
    for b in range(nb):
        cols = slice(b * dc, (b + 1) * dc)
        grad_norm = final[b, :, 1].reshape(rows, dc).astype(F32)
        grad_ref[:, cols] = (
            gain_own[:, cols] * grad_norm / rms - resid[:, cols].astype(F32) * scale
        )

    for other in range(nc):
        @pl.when(other != c)
        def _(other=other):
            loss_copy(other, other).wait_recv()
    total = loss_ctx[0]
    for other in range(1, nc):
        total = total + loss_ctx[other]
    loss_ref[...] = total[0:1, 0:1] / total[1:2, 0:1]

    for other in range(nc):
        @pl.when(other > c)
        def _(other=other):
            for copy in kv_copies(c, other):
                copy.wait_send()

        @pl.when(other != c)
        def _(other=other):
            loss_copy(c, other).wait_send()

    exchange_end(squares, sq_send, sq_recv)
    exchange_end(inner, in_send, in_recv)
    for b in range(nb):
        for other in range(nh):
            @pl.when((h * nb + b != c) | (other != h))
            def _(b=b, other=other):
                hop_one(b, other).wait_send()
    for block in range(nc):
        others(nhead, my_head, lambda g: to_head(block, h, g).wait_send())
        for g in range(nhead):
            others(npair, my_pair, lambda p: to_mate(block, g * npair + my_pair, p).wait_send())

        @pl.when((block <= c) & (c < nc - 1))
        def _(block=block):
            feats_copy(block, 0).wait_send()

        @pl.when((block >= c) & (c > 0))
        def _(block=block):
            feats_copy(block, 1).wait_send()

    others(nc, c, lambda o: keep_copy(c, o).wait_send())
    peers(lambda o: remote(loss_head.at[h], loss_head.at[h], lh_send.at[o], lh_recv.at[h], c, o).wait_send())

    def drain(j, carry):
        for block in range(nc):
            @pl.when(block > c)
            def _(block=block):
                go_right(j, block).wait_send()

            @pl.when(block < c)
            def _(block=block):
                go_left(j, block).wait_send()

            @pl.when((block <= c) & (c < nc - 1))
            def _(block=block):
                gather_copy(j, block, 0).wait_send()

            @pl.when((block >= c) & (c > 0))
            def _(block=block):
                gather_copy(j, block, 1).wait_send()

        return carry

    lax.fori_loop(0, chunks, drain, 0)
    for k in range(nc):
        others(npair, my_pair, lambda p: pair_copy(p, k, my_pair).wait_send())
        others(nhead, my_head, lambda g: head_copy(g, k, my_head).wait_send())
    for block in range(nc):
        @pl.when((block != c) | (to_h != h))
        def _(block=block):
            final_copy(block).wait_send()


def local(
    student_query, teacher_keys, teacher_values, band_span, residual_in, norm_gain,
    w_gate, w_up, w_down, teacher_feats, keep_tiles,
):
    nc, nhead, npair = (lax.axis_size(a) for a in ("ctx", "head", "pair"))
    nh = nhead * npair
    nb = nc // nh
    rows, own_cols = residual_in.shape
    sub = rows // nh
    dc, ff = w_gate.shape
    chunks = CHUNKS
    cw = ff // chunks
    kv = teacher_keys.shape[1]
    vmem = pl.BlockSpec(memory_space=pltpu.VMEM)
    hbm = pl.BlockSpec(memory_space=pl.ANY)
    dma = lambda *shape: pltpu.SemaphoreType.DMA(shape)
    kernel = functools.partial(layer_kernel, nc, nhead, npair, chunks)
    layer_out, loss, grad = pl.pallas_call(
        kernel,
        out_shape=(
            jax.ShapeDtypeStruct((rows, own_cols), BF16),
            jax.ShapeDtypeStruct((1, 1), F32),
            jax.ShapeDtypeStruct((rows, own_cols), F32),
        ),
        in_specs=[vmem] * 6 + [hbm] * 3 + [vmem] * 2,
        out_specs=(vmem, vmem, vmem),
        scratch_shapes=[
            pltpu.VMEM((dc, ff), BF16),
            pltpu.VMEM((dc, ff), BF16),
            pltpu.VMEM((ff, dc), BF16),
            pltpu.VMEM((nc, rows, kv), BF16),
            pltpu.VMEM((nc, rows, kv), BF16),
            pltpu.VMEM((rows, own_cols), BF16),
            pltpu.VMEM((nh, rows, TILE), F32),
            pltpu.VMEM((nb, nh, sub, dc), BF16),
            pltpu.VMEM((nc, nh, sub, dc), BF16),
            pltpu.VMEM((nc, rows, 2 * cw), F32),
            pltpu.VMEM((chunks, nc, rows, 2 * cw), BF16),
            pltpu.VMEM((chunks, nc, rows, 2 * cw), BF16),
            pltpu.VMEM((chunks, nc, rows, 2 * cw), BF16),
            pltpu.VMEM((chunks, rows, 2 * cw), F32),
            pltpu.VMEM((chunks, nc, rows, 2 * cw), BF16),
            pltpu.VMEM((nc, rows, dc), F32),
            pltpu.VMEM((nc, rows, dc), F32),
            pltpu.VMEM((nc, rows, ff), BF16),
            pltpu.VMEM((nc, ff // TILE, rows), jnp.int32),
            pltpu.VMEM((3, nc, rows, cw), BF16),
            pltpu.VMEM((npair, nc, nhead, 2, sub, dc), BF16),
            pltpu.VMEM((npair, nc, nhead, 2, sub, dc), BF16),
            pltpu.VMEM((nhead, nc, 2, sub, dc), BF16),
            pltpu.VMEM((nb, nh, 2, sub, dc), BF16),
            pltpu.VMEM((nh, rows, TILE), F32),
            pltpu.VMEM((nh, 8, TILE), F32),
            pltpu.VMEM((nc, 8, TILE), F32),
            pltpu.VMEM((rows, cw), F32),
            dma(3),
            dma(2, nc), dma(2, nc),
            dma(nh), dma(nh),
            dma(nb, nh), dma(nc),
            dma(nhead, nc), dma(npair, nh, nc), dma(nh, nc),
            dma(2, nc), dma(nc),
            dma(nc), dma(nc),
            dma(chunks, nc), dma(chunks, nc), dma(chunks, nc),
            dma(2, chunks, nc), dma(chunks, nc),
            dma(npair, nc), dma(npair, nc),
            dma(nhead, nc), dma(nhead, nc),
            dma(nc), dma(nb, nh),
            dma(nh), dma(nh),
            dma(nh), dma(nh),
            dma(nc), dma(nc),
        ],
        compiler_params=pltpu.CompilerParams(
            collective_id=0, has_side_effects=True, vmem_limit_bytes=60 * 1024 * 1024
        ),
        cost_estimate=pl.CostEstimate(
            flops=10 * nc * rows * dc * ff, bytes_accessed=6 * dc * ff, transcendentals=0
        ),
    )(
        student_query, teacher_keys, teacher_values, band_span.reshape(1, rows), residual_in,
        norm_gain.reshape(1, -1), w_gate, w_up, w_down, teacher_feats, keep_tiles.T,
    )
    return (layer_out, loss.reshape(1), grad)


def solution(mesh):
    in_specs = (
        P(("groups", "ctx"), ("head", "pair")),
        P(("groups", "ctx"), ("head", "pair")),
        P(("groups", "ctx"), ("head", "pair")),
        P(("groups", "ctx")),
        P(("groups", "ctx"), ("head", "pair")),
        P(),
        P("ctx", ("head", "pair")),
        P("ctx", ("head", "pair")),
        P(("head", "pair"), "ctx"),
        P(("groups", "ctx"), ("head", "pair")),
        P(("groups", "ctx"), ("head", "pair")),
    )
    out_specs = (
        P(("groups", "ctx"), ("head", "pair")),
        P("groups"),
        P(("groups", "ctx"), ("head", "pair")),
    )
    return jax.shard_map(local, mesh=mesh, in_specs=in_specs, out_specs=out_specs, check_vma=False)
```

```python
import functools
import math

import jax
import jax.numpy as jnp
from jax import lax
from jax.experimental import pallas as pl
from jax.experimental.pallas import tpu as pltpu
from jax.sharding import PartitionSpec as P

HEAD_DIM = 128
TILE = 128
CHUNKS = 7
MESH = pl.DeviceIdType.MESH
F32 = jnp.float32
BF16 = jnp.bfloat16


def layer_kernel(
    nc, nhead, npair, chunks,
    q_ref, k_ref, v_ref, span_ref, res_ref, gain_ref, wg_hbm, wu_hbm, wd_hbm, feats_ref, keep_ref,
    out_ref, loss_ref, grad_ref,
    wg, wu, wd, kbuf, vbuf, resid, squares, nbuf, xall, tmp, part, landing, own,
    gathered, acc_down, acc_grad, feats, keeps, wide_keep, terms, sums, pair_in, head_in, final, inner, loss_head,
    loss_ctx, loss_acc,
    w_sem, kv_send, kv_recv, sq_send, sq_recv, n_send, n_recv, x_send, m_send, x_recv, ft_send, ft_recv, kp_send, kp_recv, rs_send, right_recv,
    left_recv, ag_send, ag_recv, p_send, p_recv, h_send, h_recv, f_send, f_recv, in_send, in_recv,
    lh_send, lh_recv, lc_send, lc_recv,
):
    nh = nhead * npair
    nb = nc // nh
    depth = terms.shape[0]
    rows = q_ref.shape[0]
    sub = rows // nh
    dc = wg.shape[0]
    width = nc * dc
    ff = wg.shape[1]
    cw = ff // chunks
    c = lax.axis_index("ctx")
    my_head = lax.axis_index("head")
    my_pair = lax.axis_index("pair")
    h = my_head * npair + my_pair

    def remote(src, dst, send, recv, to_c, to_h):
        return pltpu.make_async_remote_copy(
            src_ref=src, dst_ref=dst, send_sem=send, recv_sem=recv,
            device_id={"ctx": to_c, "head": to_h // npair, "pair": to_h % npair},
            device_id_type=MESH,
        )

    weight_copies = [
        pltpu.make_async_copy(a, b, w_sem.at[i])
        for i, (a, b) in enumerate(((wg_hbm, wg), (wu_hbm, wu), (wd_hbm, wd)))
    ]
    for copy in weight_copies:
        copy.start()

    barrier = pltpu.get_barrier_semaphore()

    def greet(i, carry):
        to_c, to_h = i // nh, i % nh

        @pl.when((to_c != c) | (to_h != h))
        def _():
            pl.semaphore_signal(
                barrier, inc=1,
                device_id={"ctx": to_c, "head": to_h // npair, "pair": to_h % npair},
                device_id_type=MESH,
            )

        return carry

    lax.fori_loop(0, nc * nh, greet, 0)
    pl.semaphore_wait(barrier, nc * nh - 1)

    def kv_copies(block, to_c):
        return (
            remote(kbuf.at[block], kbuf.at[block], kv_send.at[0, to_c], kv_recv.at[0, block], to_c, h),
            remote(vbuf.at[block], vbuf.at[block], kv_send.at[1, to_c], kv_recv.at[1, block], to_c, h),
        )

    keeps[c] = keep_ref[...]

    def keep_copy(block, to_c):
        return remote(keeps.at[block], keeps.at[block], kp_send.at[to_c], kp_recv.at[block], to_c, h)

    for other in range(nc):
        @pl.when(other != c)
        def _(other=other):
            keep_copy(c, other).start()
    kbuf[c] = k_ref[...]
    vbuf[c] = v_ref[...]
    for other in range(nc):
        @pl.when(other > c)
        def _(other=other):
            for copy in kv_copies(c, other):
                copy.start()
            kbuf[other] = jnp.zeros_like(k_ref)
            vbuf[other] = jnp.zeros_like(v_ref)
    own_cols = res_ref.shape[1]
    gain_own = gain_ref[:, pl.ds(pl.multiple_of(h * own_cols, TILE), own_cols)]
    feats[c] = feats_ref[...]

    def feats_copy(block, direction):
        to_c = lax.rem(c + 1, nc) if direction == 0 else lax.rem(c + nc - 1, nc)
        return remote(
            feats.at[block], feats.at[block], ft_send.at[direction, block], ft_recv.at[block], to_c, h
        )

    def feats_forward(far):
        @pl.when(c >= far)
        def _():
            block = lax.rem(c - far + nc, nc)
            feats_copy(block, 0).wait_recv()

            @pl.when(c < nc - 1)
            def _():
                feats_copy(block, 0).start()

        @pl.when(c + far < nc)
        def _():
            block = lax.rem(c + far, nc)
            feats_copy(block, 1).wait_recv()

            @pl.when(c > 0)
            def _():
                feats_copy(block, 1).start()

    for other in range(nc):
        @pl.when(other != c)
        def _(other=other):
            keep_copy(other, other).wait_recv()

    def widen(block, carry):
        for t in range(ff // TILE):
            wide_keep[block, :, t * TILE : (t + 1) * TILE] = jnp.transpose(
                jnp.broadcast_to(keeps[block, t : t + 1, :].astype(F32), (TILE, rows))
            ).astype(BF16)
        return carry

    lax.fori_loop(0, nc, widen, 0)
    for other in range(nc):
        @pl.when(other < c)
        def _(other=other):
            for copy in kv_copies(other, c):
                copy.wait_recv()

    @pl.when(c < nc - 1)
    def _():
        feats_copy(c, 0).start()

    @pl.when(c > 0)
    def _():
        feats_copy(c, 1).start()

    span_of = jnp.transpose(jnp.broadcast_to(span_ref[...].astype(F32), (TILE, rows)))[:, :1]
    span_of = span_of.astype(jnp.int32)
    span = nc * rows
    key_pos = lax.broadcasted_iota(jnp.int32, (rows, span), 1)
    query_pos = c * rows + lax.broadcasted_iota(jnp.int32, (rows, span), 0)
    distance = query_pos - key_pos
    allowed = (distance >= 0) & (distance < span_of)
    kv_heads = k_ref.shape[1] // HEAD_DIM
    heads = q_ref.shape[1] // HEAD_DIM
    per = heads // kv_heads
    for kv in range(kv_heads):
        kcols = slice(kv * HEAD_DIM, (kv + 1) * HEAD_DIM)
        keys = kbuf[:, :, kcols].reshape(span, HEAD_DIM)
        values = vbuf[:, :, kcols].reshape(span, HEAD_DIM)
        for a in range(kv * per, (kv + 1) * per):
            cols = slice(a * HEAD_DIM, (a + 1) * HEAD_DIM)
            scores = lax.dot_general(
                q_ref[:, cols], keys, (((1,), (1,)), ((), ())), preferred_element_type=F32
            ) * (1.0 / math.sqrt(HEAD_DIM))
            masked = jnp.where(allowed, scores, -jnp.inf)
            weights = jnp.exp(masked - jnp.max(masked, axis=-1, keepdims=True))
            probs = (weights / jnp.sum(weights, axis=-1, keepdims=True)).astype(BF16)
            attended = jnp.dot(probs, values, preferred_element_type=F32)
            resid[:, cols] = (res_ref[:, cols].astype(F32) + attended).astype(BF16)

    def peers(body):
        for other in range(nh):
            @pl.when(other != h)
            def _(other=other):
                body(other)

    def exchange(buf, send, recv):
        peers(lambda o: remote(buf.at[h], buf.at[h], send.at[o], recv.at[h], c, o).start())
        peers(lambda o: remote(buf.at[o], buf.at[o], send.at[o], recv.at[o], c, o).wait_recv())
        total = buf[0]
        for other in range(1, nh):
            total = total + buf[other]
        return total

    def exchange_end(buf, send, recv):
        peers(lambda o: remote(buf.at[h], buf.at[h], send.at[o], recv.at[h], c, o).wait_send())

    resid_own = resid[...].astype(F32)
    squares[h] = jnp.broadcast_to(
        jnp.sum(resid_own * resid_own, axis=1, keepdims=True), (rows, TILE)
    )
    rms = jnp.sqrt(exchange(squares, sq_send, sq_recv)[:, :1] / width + 1e-05)

    normed = (resid[...].astype(F32) / rms * gain_own).astype(BF16)
    for b in range(nb):
        nbuf[b] = normed[:, b * dc : (b + 1) * dc].reshape(nh, sub, dc)

    def hop_one(b, other):
        to_c = h * nb + b
        return remote(
            nbuf.at[b, other], xall.at[c, other], n_send.at[b, other], n_recv.at[c], to_c, other
        )

    for b in range(nb):
        for other in range(nh):
            mine = (h * nb + b == c) & (other == h)

            @pl.when(jnp.logical_not(mine))
            def _(b=b, other=other):
                hop_one(b, other).start()

            @pl.when(mine)
            def _(b=b, other=other):
                xall[c, other] = nbuf[b, other]

    source_h = c // nb

    def to_head(block, row_h, g):
        return remote(
            xall.at[block, row_h], xall.at[block, row_h], x_send.at[g, block],
            x_recv.at[row_h, block], c, g * npair + my_pair,
        )

    def to_mate(block, row_h, p):
        return remote(
            xall.at[block, row_h], xall.at[block, row_h], m_send.at[p, row_h, block],
            x_recv.at[row_h, block], c, my_head * npair + p,
        )

    def others(count, mine, body):
        for o in range(count):
            @pl.when(o != mine)
            def _(o=o):
                body(o)

    for k in range(nc):
        block = lax.rem(c + k, nc)

        @pl.when((block != c) | (source_h != h))
        def _(block=block):
            remote(
                xall.at[block, h], xall.at[block, h], n_send.at[0, 0], n_recv.at[block],
                block, source_h,
            ).wait_recv()

        others(nhead, my_head, lambda g: to_head(block, h, g).start())
        others(npair, my_pair, lambda p: to_mate(block, h, p).start())
    feats_forward(1)
    for k in range(nc):
        block = lax.rem(c + k, nc)

        def pass_on(g):
            row_h = g * npair + my_pair
            to_head(block, row_h, g).wait_recv()
            others(npair, my_pair, lambda p: to_mate(block, row_h, p).start())

        others(nhead, my_head, pass_on)
    for copy in weight_copies:
        copy.wait()
    for k in range(nc):
        for g in range(nhead):
            others(
                npair, my_pair, lambda p: to_mate(k, g * npair + p, p).wait_recv()
            )

    def cols_of(j):
        return pl.ds(pl.multiple_of(j * cw, cw), cw)

    def rs_copy(j, dest, to_c, slot, recv):
        return remote(
            part.at[j, dest], landing.at[j, slot], rs_send.at[j, dest], recv.at[j, dest], to_c, h
        )

    def go_right(j, dest):
        return rs_copy(j, dest, lax.rem(c + 1, nc), dest + 1, right_recv)

    def go_left(j, dest):
        return rs_copy(j, dest, lax.rem(c + nc - 1, nc), dest, left_recv)

    group = min(nc, 4)

    def multiply(j):
        def block(i, carry):
            at = pl.ds(i * group, group)
            x = xall[at].reshape(group * rows, dc)
            for k, w in enumerate((wg, wu)):
                cols = slice(k * cw, (k + 1) * cw)
                y = jnp.dot(x, w[:, cols_of(j)], preferred_element_type=F32)
                tmp[at, :, cols] = y.reshape(group, rows, cw)
                part[j, at, :, cols] = y.astype(BF16).reshape(group, rows, cw)
            return carry

        lax.fori_loop(0, nc // group, block, 0)
        own[j] = tmp[c]

    def edge_send(j):
        for far in range(nc - 1):
            @pl.when(c == 0)
            def _(far=far):
                go_right(j, nc - 1 - far).start()

            @pl.when(c == nc - 1)
            def _(far=far):
                go_left(j, far).start()

    def reduce_right(j):
        for far in range(nc - 2):
            dest = nc - 1 - far

            @pl.when(c < dest)
            def _(dest=dest):
                go_right(j, dest).wait_recv()
                part[j, dest] = (part[j, dest].astype(F32) + landing[j, dest + 1].astype(F32)).astype(BF16)
                go_right(j, dest).start()

    def reduce_left(j):
        for dest in range(nc - 2):
            @pl.when(c > dest)
            def _(dest=dest):
                go_left(j, dest).wait_recv()
                part[j, dest] = (part[j, dest].astype(F32) + landing[j, dest].astype(F32)).astype(BF16)
                go_left(j, dest).start()

    def gather_copy(j, block, direction):
        to_c = lax.rem(c + 1, nc) if direction == 0 else lax.rem(c + nc - 1, nc)
        return remote(
            gathered.at[j, block], gathered.at[j, block], ag_send.at[direction, j, block],
            ag_recv.at[j, block], to_c, h,
        )

    loss_acc[...] = jnp.zeros_like(loss_acc)
    def keep_of(j, block):
        return wide_keep[block, :, cols_of(j)].astype(F32)

    def derive(j, i):
        gate = gathered[j, i, :, 0:cw].astype(F32)
        up = gathered[j, i, :, cw : 2 * cw].astype(F32)
        lifted = jnp.maximum(gate, 0.0)
        squared = lifted * lifted
        act = squared * up
        differ = act - feats[i, :, cols_of(j)].astype(F32)
        grad_act = keep_of(j, i) * differ
        at = lax.rem(j, depth)
        terms[at, 0, i] = act.astype(BF16)
        terms[at, 1, i] = (grad_act * up * 2.0 * lifted).astype(BF16)
        terms[at, 2, i] = (grad_act * squared).astype(BF16)

    def features(j):
        @pl.when(c > 0)
        def _():
            go_right(j, c).wait_recv()
            own[j] = own[j] + landing[j, c + 1].astype(F32)

        @pl.when(c < nc - 1)
        def _():
            go_left(j, c).wait_recv()
            own[j] = own[j] + landing[j, c].astype(F32)

        gate = own[j, :, 0:cw]
        up = own[j, :, cw : 2 * cw]
        lifted = jnp.maximum(gate, 0.0)
        squared = lifted * lifted
        act = squared * up
        differ = act - feats_ref[:, cols_of(j)].astype(F32)
        loss_acc[...] += keep_of(j, c) * differ * differ
        gathered[j, c] = own[j].astype(BF16)

        @pl.when(c < nc - 1)
        def _():
            gather_copy(j, c, 0).start()

        @pl.when(c > 0)
        def _():
            gather_copy(j, c, 1).start()

        derive(j, c)

    def forward(j, far):
        @pl.when(c >= far)
        def _():
            block = lax.rem(c - far + nc, nc)
            gather_copy(j, block, 0).wait_recv()

            @pl.when(c < nc - 1)
            def _():
                gather_copy(j, block, 0).start()

            derive(j, block)

        @pl.when(c + far < nc)
        def _():
            block = lax.rem(c + far, nc)
            gather_copy(j, block, 1).wait_recv()

            @pl.when(c > 0)
            def _():
                gather_copy(j, block, 1).start()

            derive(j, block)

    contract = (((1,), (1,)), ((), ()))
    acc_down[...] = jnp.zeros_like(acc_down)
    acc_grad[...] = jnp.zeros_like(acc_grad)

    def accumulate(j):
        def block(i, carry):
            at = pl.ds(i * group, group)

            def rows_of(k):
                return terms[lax.rem(j, depth), k, at].reshape(group * rows, cw)

            down = jnp.dot(rows_of(0), wd[cols_of(j), :], preferred_element_type=F32)
            acc_down[at] += down.reshape(group, rows, dc)
            grad = lax.dot_general(
                rows_of(1), wg[:, cols_of(j)], contract, preferred_element_type=F32
            ) + lax.dot_general(rows_of(2), wu[:, cols_of(j)], contract, preferred_element_type=F32)
            acc_grad[at] += grad.reshape(group, rows, dc)
            return carry

        lax.fori_loop(0, nc // group, block, 0)

    ahead = 2
    feature_lag = max(nc - 2, 1)
    inside = (c > 0) & (c < nc - 1)

    def step(i, carry):
        def when(lag, body, also=True):
            j = i - lag

            @pl.when((j >= 0) & (j < chunks) & also)
            def _():
                body(j)

        @pl.when(i < nc - 2)
        def _():
            feats_forward(i + 2)

        when(-ahead, multiply)
        when(c - 1, reduce_right, inside)
        when(nc - 2 - c, reduce_left, inside)
        when(feature_lag, features)
        for far in range(1, nc):
            when(feature_lag + far, functools.partial(forward, far=far))
        when(-1, edge_send)
        when(feature_lag + nc - 1, accumulate)
        return carry

    multiply(0)
    edge_send(0)
    multiply(1)
    lax.fori_loop(0, chunks + feature_lag + nc - 1, step, 0)

    loss_part = jnp.sum(jnp.sum(loss_acc[...], axis=1, keepdims=True), axis=0, keepdims=True)
    count_part = jnp.sum(
        jnp.sum(keep_ref[...].astype(F32), axis=1, keepdims=True), axis=0, keepdims=True
    ) * TILE
    line = lax.broadcasted_iota(jnp.int32, (8, TILE), 0)
    loss_head[h] = jnp.where(line == 0, loss_part, count_part)
    peers(lambda o: remote(loss_head.at[h], loss_head.at[h], lh_send.at[o], lh_recv.at[h], c, o).start())

    def pair_copy(p, k, slot):
        return remote(
            sums.at[p, k], pair_in.at[slot, k], p_send.at[p, k], p_recv.at[slot, k],
            c, my_head * npair + p,
        )

    for k in range(nc):
        for p in range(npair):
            for g in range(nhead):
                o = g * npair + p
                sums[p, k, g, 0] = acc_down[k, o * sub : (o + 1) * sub].astype(BF16)
                sums[p, k, g, 1] = acc_grad[k, o * sub : (o + 1) * sub].astype(BF16)
        others(npair, my_pair, lambda p: pair_copy(p, k, my_pair).start())

    def head_copy(g, k, slot):
        return remote(
            sums.at[my_pair, k, g], head_in.at[slot, k], h_send.at[g, k], h_recv.at[slot, k],
            c, g * npair + my_pair,
        )

    for k in range(nc):
        def add_pair(p):
            pair_copy(p, k, p).wait_recv()
            sums[my_pair, k] = (
                sums[my_pair, k].astype(F32) + pair_in[p, k].astype(F32)
            ).astype(BF16)

        others(npair, my_pair, add_pair)
        others(nhead, my_head, lambda g: head_copy(g, k, my_head).start())

    peers(lambda o: remote(loss_head.at[o], loss_head.at[o], lh_send.at[o], lh_recv.at[o], c, o).wait_recv())
    head_total = loss_head[0]
    for other in range(1, nh):
        head_total = head_total + loss_head[other]
    loss_ctx[c] = head_total

    def loss_copy(block, to_c):
        return remote(
            loss_ctx.at[block], loss_ctx.at[block], lc_send.at[to_c], lc_recv.at[block], to_c, h
        )

    for other in range(nc):
        @pl.when(other != c)
        def _(other=other):
            loss_copy(c, other).start()

    to_h = c // nb
    slot = lax.rem(c, nb) if nb > 1 else 0

    def final_copy(block):
        return remote(
            sums.at[my_pair, block, my_head], final.at[slot, h], f_send.at[block],
            f_recv.at[slot, h], block, to_h,
        )

    for block in range(nc):
        def add_head(g):
            head_copy(g, block, g).wait_recv()
            sums[my_pair, block, my_head] = (
                sums[my_pair, block, my_head].astype(F32) + head_in[g, block].astype(F32)
            ).astype(BF16)

        others(nhead, my_head, add_head)
        mine = (block == c) & (to_h == h)

        @pl.when(jnp.logical_not(mine))
        def _(block=block):
            final_copy(block).start()

        @pl.when(mine)
        def _(block=block):
            final[slot, h] = sums[my_pair, block, my_head]

    for b in range(nb):
        for other in range(nh):
            from_c = h * nb + b

            @pl.when((from_c != c) | (other != h))
            def _(b=b, other=other, from_c=from_c):
                remote(
                    final.at[b, other], final.at[b, other], f_send.at[0], f_recv.at[b, other],
                    from_c, other,
                ).wait_recv()

    inner_part = jnp.zeros((rows, 1), F32)
    for b in range(nb):
        cols = slice(b * dc, (b + 1) * dc)
        down = final[b, :, 0].reshape(rows, dc).astype(F32)
        out_ref[:, cols] = (resid[:, cols].astype(F32) + down).astype(BF16)
        grad_norm = final[b, :, 1].reshape(rows, dc).astype(F32)
        inner_part += jnp.sum(
            gain_own[:, cols] * grad_norm * resid[:, cols].astype(F32), axis=1, keepdims=True
        )
    inner[h] = jnp.broadcast_to(inner_part, (rows, TILE))
    inner_sum = exchange(inner, in_send, in_recv)[:, :1]
    rms = jnp.sqrt(
        functools.reduce(lambda a, b: a + b, [squares[o] for o in range(nh)])[:, :1] / width + 1e-05
    )
    scale = inner_sum / (width * (rms * rms * rms))
    for b in range(nb):
        cols = slice(b * dc, (b + 1) * dc)
        grad_norm = final[b, :, 1].reshape(rows, dc).astype(F32)
        grad_ref[:, cols] = (
            gain_own[:, cols] * grad_norm / rms - resid[:, cols].astype(F32) * scale
        )

    for other in range(nc):
        @pl.when(other != c)
        def _(other=other):
            loss_copy(other, other).wait_recv()
    total = loss_ctx[0]
    for other in range(1, nc):
        total = total + loss_ctx[other]
    loss_ref[...] = total[0:1, 0:1] / total[1:2, 0:1]

    for other in range(nc):
        @pl.when(other > c)
        def _(other=other):
            for copy in kv_copies(c, other):
                copy.wait_send()

        @pl.when(other != c)
        def _(other=other):
            loss_copy(c, other).wait_send()

    exchange_end(squares, sq_send, sq_recv)
    exchange_end(inner, in_send, in_recv)
    for b in range(nb):
        for other in range(nh):
            @pl.when((h * nb + b != c) | (other != h))
            def _(b=b, other=other):
                hop_one(b, other).wait_send()
    for block in range(nc):
        others(nhead, my_head, lambda g: to_head(block, h, g).wait_send())
        for g in range(nhead):
            others(npair, my_pair, lambda p: to_mate(block, g * npair + my_pair, p).wait_send())

        @pl.when((block <= c) & (c < nc - 1))
        def _(block=block):
            feats_copy(block, 0).wait_send()

        @pl.when((block >= c) & (c > 0))
        def _(block=block):
            feats_copy(block, 1).wait_send()

    others(nc, c, lambda o: keep_copy(c, o).wait_send())
    peers(lambda o: remote(loss_head.at[h], loss_head.at[h], lh_send.at[o], lh_recv.at[h], c, o).wait_send())

    def drain(j, carry):
        for block in range(nc):
            @pl.when(block > c)
            def _(block=block):
                go_right(j, block).wait_send()

            @pl.when(block < c)
            def _(block=block):
                go_left(j, block).wait_send()

            @pl.when((block <= c) & (c < nc - 1))
            def _(block=block):
                gather_copy(j, block, 0).wait_send()

            @pl.when((block >= c) & (c > 0))
            def _(block=block):
                gather_copy(j, block, 1).wait_send()

        return carry

    lax.fori_loop(0, chunks, drain, 0)
    for k in range(nc):
        others(npair, my_pair, lambda p: pair_copy(p, k, my_pair).wait_send())
        others(nhead, my_head, lambda g: head_copy(g, k, my_head).wait_send())
    for block in range(nc):
        @pl.when((block != c) | (to_h != h))
        def _(block=block):
            final_copy(block).wait_send()


def local(
    student_query, teacher_keys, teacher_values, band_span, residual_in, norm_gain,
    w_gate, w_up, w_down, teacher_feats, keep_tiles,
):
    nc, nhead, npair = (lax.axis_size(a) for a in ("ctx", "head", "pair"))
    nh = nhead * npair
    nb = nc // nh
    rows, own_cols = residual_in.shape
    sub = rows // nh
    dc, ff = w_gate.shape
    chunks = CHUNKS
    cw = ff // chunks
    kv = teacher_keys.shape[1]
    vmem = pl.BlockSpec(memory_space=pltpu.VMEM)
    hbm = pl.BlockSpec(memory_space=pl.ANY)
    dma = lambda *shape: pltpu.SemaphoreType.DMA(shape)
    kernel = functools.partial(layer_kernel, nc, nhead, npair, chunks)
    layer_out, loss, grad = pl.pallas_call(
        kernel,
        out_shape=(
            jax.ShapeDtypeStruct((rows, own_cols), BF16),
            jax.ShapeDtypeStruct((1, 1), F32),
            jax.ShapeDtypeStruct((rows, own_cols), F32),
        ),
        in_specs=[vmem] * 6 + [hbm] * 3 + [vmem] * 2,
        out_specs=(vmem, vmem, vmem),
        scratch_shapes=[
            pltpu.VMEM((dc, ff), BF16),
            pltpu.VMEM((dc, ff), BF16),
            pltpu.VMEM((ff, dc), BF16),
            pltpu.VMEM((nc, rows, kv), BF16),
            pltpu.VMEM((nc, rows, kv), BF16),
            pltpu.VMEM((rows, own_cols), BF16),
            pltpu.VMEM((nh, rows, TILE), F32),
            pltpu.VMEM((nb, nh, sub, dc), BF16),
            pltpu.VMEM((nc, nh, sub, dc), BF16),
            pltpu.VMEM((nc, rows, 2 * cw), F32),
            pltpu.VMEM((chunks, nc, rows, 2 * cw), BF16),
            pltpu.VMEM((chunks, nc + 1, rows, 2 * cw), BF16),
            pltpu.VMEM((chunks, rows, 2 * cw), F32),
            pltpu.VMEM((chunks, nc, rows, 2 * cw), BF16),
            pltpu.VMEM((nc, rows, dc), F32),
            pltpu.VMEM((nc, rows, dc), F32),
            pltpu.VMEM((nc, rows, ff), BF16),
            pltpu.VMEM((nc, ff // TILE, rows), jnp.int32),
            pltpu.VMEM((nc, rows, ff), BF16),
            pltpu.VMEM((min(chunks, nc), 3, nc, rows, cw), BF16),
            pltpu.VMEM((npair, nc, nhead, 2, sub, dc), BF16),
            pltpu.VMEM((npair, nc, nhead, 2, sub, dc), BF16),
            pltpu.VMEM((nhead, nc, 2, sub, dc), BF16),
            pltpu.VMEM((nb, nh, 2, sub, dc), BF16),
            pltpu.VMEM((nh, rows, TILE), F32),
            pltpu.VMEM((nh, 8, TILE), F32),
            pltpu.VMEM((nc, 8, TILE), F32),
            pltpu.VMEM((rows, cw), F32),
            dma(3),
            dma(2, nc), dma(2, nc),
            dma(nh), dma(nh),
            dma(nb, nh), dma(nc),
            dma(nhead, nc), dma(npair, nh, nc), dma(nh, nc),
            dma(2, nc), dma(nc),
            dma(nc), dma(nc),
            dma(chunks, nc), dma(chunks, nc), dma(chunks, nc),
            dma(2, chunks, nc), dma(chunks, nc),
            dma(npair, nc), dma(npair, nc),
            dma(nhead, nc), dma(nhead, nc),
            dma(nc), dma(nb, nh),
            dma(nh), dma(nh),
            dma(nh), dma(nh),
            dma(nc), dma(nc),
        ],
        compiler_params=pltpu.CompilerParams(
            collective_id=0, has_side_effects=True, vmem_limit_bytes=60 * 1024 * 1024
        ),
        cost_estimate=pl.CostEstimate(
            flops=10 * nc * rows * dc * ff, bytes_accessed=6 * dc * ff, transcendentals=0
        ),
    )(
        student_query, teacher_keys, teacher_values, band_span.reshape(1, rows), residual_in,
        norm_gain.reshape(1, -1), w_gate, w_up, w_down, teacher_feats, keep_tiles.T,
    )
    return (layer_out, loss.reshape(1), grad)


def solution(mesh):
    in_specs = (
        P(("groups", "ctx"), ("head", "pair")),
        P(("groups", "ctx"), ("head", "pair")),
        P(("groups", "ctx"), ("head", "pair")),
        P(("groups", "ctx")),
        P(("groups", "ctx"), ("head", "pair")),
        P(),
        P("ctx", ("head", "pair")),
        P("ctx", ("head", "pair")),
        P(("head", "pair"), "ctx"),
        P(("groups", "ctx"), ("head", "pair")),
        P(("groups", "ctx"), ("head", "pair")),
    )
    out_specs = (
        P(("groups", "ctx"), ("head", "pair")),
        P("groups"),
        P(("groups", "ctx"), ("head", "pair")),
    )
    return jax.shard_map(local, mesh=mesh, in_specs=in_specs, out_specs=out_specs, check_vma=False)
```

```python
import functools
import math

import jax
import jax.numpy as jnp
from jax import lax
from jax.experimental import pallas as pl
from jax.experimental.pallas import tpu as pltpu
from jax.sharding import PartitionSpec as P

HEAD_DIM = 128
TILE = 128
CHUNKS = 7
MESH = pl.DeviceIdType.MESH
F32 = jnp.float32
BF16 = jnp.bfloat16


def layer_kernel(
    nc, nhead, npair, chunks,
    q_ref, k_ref, v_ref, span_ref, res_ref, gain_ref, wg_hbm, wu_hbm, wd_hbm, feats_ref, keep_ref,
    out_ref, loss_ref, grad_ref,
    wg, wu, wd, kbuf, vbuf, resid, squares, nbuf, xall, tmp, part, landing, own,
    gathered, acc_down, acc_grad, feats, keeps, wide_keep, terms, sums, pair_in, head_in, final, inner, loss_head,
    loss_ctx, loss_acc,
    w_sem, kv_send, kv_recv, sq_send, sq_recv, n_send, n_recv, x_send, m_send, x_recv, ft_send, ft_recv, kp_send, kp_recv, rs_send, right_recv,
    left_recv, ag_send, ag_recv, p_send, p_recv, h_send, h_recv, f_send, f_recv, in_send, in_recv,
    lh_send, lh_recv, lc_send, lc_recv,
):
    nh = nhead * npair
    nb = nc // nh
    depth = terms.shape[0]
    rows = q_ref.shape[0]
    sub = rows // nh
    dc = wg.shape[0]
    width = nc * dc
    ff = wg.shape[1]
    cw = ff // chunks
    c = lax.axis_index("ctx")
    my_head = lax.axis_index("head")
    my_pair = lax.axis_index("pair")
    h = my_head * npair + my_pair

    def remote(src, dst, send, recv, to_c, to_h):
        return pltpu.make_async_remote_copy(
            src_ref=src, dst_ref=dst, send_sem=send, recv_sem=recv,
            device_id={"ctx": to_c, "head": to_h // npair, "pair": to_h % npair},
            device_id_type=MESH,
        )

    weight_copies = [
        pltpu.make_async_copy(a, b, w_sem.at[i])
        for i, (a, b) in enumerate(((wg_hbm, wg), (wu_hbm, wu), (wd_hbm, wd)))
    ]
    for copy in weight_copies:
        copy.start()

    barrier = pltpu.get_barrier_semaphore()

    def greet(i, carry):
        to_c, to_h = i // nh, i % nh

        @pl.when((to_c != c) | (to_h != h))
        def _():
            pl.semaphore_signal(
                barrier, inc=1,
                device_id={"ctx": to_c, "head": to_h // npair, "pair": to_h % npair},
                device_id_type=MESH,
            )

        return carry

    lax.fori_loop(0, nc * nh, greet, 0)
    pl.semaphore_wait(barrier, nc * nh - 1)

    def kv_copies(block, to_c):
        return (
            remote(kbuf.at[block], kbuf.at[block], kv_send.at[0, to_c], kv_recv.at[0, block], to_c, h),
            remote(vbuf.at[block], vbuf.at[block], kv_send.at[1, to_c], kv_recv.at[1, block], to_c, h),
        )

    keeps[c] = keep_ref[...]

    def keep_copy(block, to_c):
        return remote(keeps.at[block], keeps.at[block], kp_send.at[to_c], kp_recv.at[block], to_c, h)

    for other in range(nc):
        @pl.when(other != c)
        def _(other=other):
            keep_copy(c, other).start()
    kbuf[c] = k_ref[...]
    vbuf[c] = v_ref[...]
    for other in range(nc):
        @pl.when(other > c)
        def _(other=other):
            for copy in kv_copies(c, other):
                copy.start()
            kbuf[other] = jnp.zeros_like(k_ref)
            vbuf[other] = jnp.zeros_like(v_ref)
    own_cols = res_ref.shape[1]
    gain_own = gain_ref[:, pl.ds(pl.multiple_of(h * own_cols, TILE), own_cols)]
    feats[c] = feats_ref[...]

    def feats_copy(block, direction):
        to_c = lax.rem(c + 1, nc) if direction == 0 else lax.rem(c + nc - 1, nc)
        return remote(
            feats.at[block], feats.at[block], ft_send.at[direction, block], ft_recv.at[block], to_c, h
        )

    def feats_forward(far):
        @pl.when(c >= far)
        def _():
            block = lax.rem(c - far + nc, nc)
            feats_copy(block, 0).wait_recv()

            @pl.when(c < nc - 1)
            def _():
                feats_copy(block, 0).start()

        @pl.when(c + far < nc)
        def _():
            block = lax.rem(c + far, nc)
            feats_copy(block, 1).wait_recv()

            @pl.when(c > 0)
            def _():
                feats_copy(block, 1).start()

    for other in range(nc):
        @pl.when(other != c)
        def _(other=other):
            keep_copy(other, other).wait_recv()

    def widen(block, carry):
        for t in range(ff // TILE):
            wide_keep[block, :, t * TILE : (t + 1) * TILE] = jnp.transpose(
                jnp.broadcast_to(keeps[block, t : t + 1, :].astype(F32), (TILE, rows))
            ).astype(BF16)
        return carry

    lax.fori_loop(0, nc, widen, 0)
    for other in range(nc):
        @pl.when(other < c)
        def _(other=other):
            for copy in kv_copies(other, c):
                copy.wait_recv()

    @pl.when(c < nc - 1)
    def _():
        feats_copy(c, 0).start()

    @pl.when(c > 0)
    def _():
        feats_copy(c, 1).start()

    span_of = jnp.transpose(jnp.broadcast_to(span_ref[...].astype(F32), (TILE, rows)))[:, :1]
    span_of = span_of.astype(jnp.int32)
    span = nc * rows
    key_pos = lax.broadcasted_iota(jnp.int32, (rows, span), 1)
    query_pos = c * rows + lax.broadcasted_iota(jnp.int32, (rows, span), 0)
    distance = query_pos - key_pos
    allowed = (distance >= 0) & (distance < span_of)
    kv_heads = k_ref.shape[1] // HEAD_DIM
    heads = q_ref.shape[1] // HEAD_DIM
    per = heads // kv_heads
    for kv in range(kv_heads):
        kcols = slice(kv * HEAD_DIM, (kv + 1) * HEAD_DIM)
        keys = kbuf[:, :, kcols].reshape(span, HEAD_DIM)
        values = vbuf[:, :, kcols].reshape(span, HEAD_DIM)
        for a in range(kv * per, (kv + 1) * per):
            cols = slice(a * HEAD_DIM, (a + 1) * HEAD_DIM)
            scores = lax.dot_general(
                q_ref[:, cols], keys, (((1,), (1,)), ((), ())), preferred_element_type=F32
            ) * (1.0 / math.sqrt(HEAD_DIM))
            masked = jnp.where(allowed, scores, -jnp.inf)
            weights = jnp.exp(masked - jnp.max(masked, axis=-1, keepdims=True))
            probs = (weights / jnp.sum(weights, axis=-1, keepdims=True)).astype(BF16)
            attended = jnp.dot(probs, values, preferred_element_type=F32)
            resid[:, cols] = (res_ref[:, cols].astype(F32) + attended).astype(BF16)

    def peers(body):
        for other in range(nh):
            @pl.when(other != h)
            def _(other=other):
                body(other)

    def exchange(buf, send, recv):
        peers(lambda o: remote(buf.at[h], buf.at[h], send.at[o], recv.at[h], c, o).start())
        peers(lambda o: remote(buf.at[o], buf.at[o], send.at[o], recv.at[o], c, o).wait_recv())
        total = buf[0]
        for other in range(1, nh):
            total = total + buf[other]
        return total

    def exchange_end(buf, send, recv):
        peers(lambda o: remote(buf.at[h], buf.at[h], send.at[o], recv.at[h], c, o).wait_send())

    resid_own = resid[...].astype(F32)
    squares[h] = jnp.broadcast_to(
        jnp.sum(resid_own * resid_own, axis=1, keepdims=True), (rows, TILE)
    )
    rms = jnp.sqrt(exchange(squares, sq_send, sq_recv)[:, :1] / width + 1e-05)

    normed = (resid[...].astype(F32) / rms * gain_own).astype(BF16)
    for b in range(nb):
        nbuf[b] = normed[:, b * dc : (b + 1) * dc].reshape(nh, sub, dc)

    def hop_one(b, other):
        to_c = h * nb + b
        return remote(
            nbuf.at[b, other], xall.at[c, other], n_send.at[b, other], n_recv.at[c], to_c, other
        )

    for b in range(nb):
        for other in range(nh):
            mine = (h * nb + b == c) & (other == h)

            @pl.when(jnp.logical_not(mine))
            def _(b=b, other=other):
                hop_one(b, other).start()

            @pl.when(mine)
            def _(b=b, other=other):
                xall[c, other] = nbuf[b, other]

    source_h = c // nb

    def to_head(block, row_h, g):
        return remote(
            xall.at[block, row_h], xall.at[block, row_h], x_send.at[g, block],
            x_recv.at[row_h, block], c, g * npair + my_pair,
        )

    def to_mate(block, row_h, p):
        return remote(
            xall.at[block, row_h], xall.at[block, row_h], m_send.at[p, row_h, block],
            x_recv.at[row_h, block], c, my_head * npair + p,
        )

    def others(count, mine, body):
        for o in range(count):
            @pl.when(o != mine)
            def _(o=o):
                body(o)

    for k in range(nc):
        block = lax.rem(c + k, nc)

        @pl.when((block != c) | (source_h != h))
        def _(block=block):
            remote(
                xall.at[block, h], xall.at[block, h], n_send.at[0, 0], n_recv.at[block],
                block, source_h,
            ).wait_recv()

        others(nhead, my_head, lambda g: to_head(block, h, g).start())
        others(npair, my_pair, lambda p: to_mate(block, h, p).start())
    feats_forward(1)
    for k in range(nc):
        block = lax.rem(c + k, nc)

        def pass_on(g):
            row_h = g * npair + my_pair
            to_head(block, row_h, g).wait_recv()
            others(npair, my_pair, lambda p: to_mate(block, row_h, p).start())

        others(nhead, my_head, pass_on)
    for copy in weight_copies:
        copy.wait()
    for k in range(nc):
        for g in range(nhead):
            others(
                npair, my_pair, lambda p: to_mate(k, g * npair + p, p).wait_recv()
            )

    def cols_of(j):
        return pl.ds(pl.multiple_of(j * cw, cw), cw)

    def rs_copy(j, dest, to_c, slot, recv):
        return remote(
            part.at[j, dest], landing.at[j, slot], rs_send.at[j, dest], recv.at[j, dest], to_c, h
        )

    def go_right(j, dest):
        return rs_copy(j, dest, lax.rem(c + 1, nc), dest + 1, right_recv)

    def go_left(j, dest):
        return rs_copy(j, dest, lax.rem(c + nc - 1, nc), dest, left_recv)

    group = min(nc, 4)

    def multiply(j):
        def block(i, carry):
            at = pl.ds(i * group, group)
            x = xall[at].reshape(group * rows, dc)
            for k, w in enumerate((wg, wu)):
                cols = slice(k * cw, (k + 1) * cw)
                y = jnp.dot(x, w[:, cols_of(j)], preferred_element_type=F32)
                tmp[at, :, cols] = y.reshape(group, rows, cw)
                part[j, at, :, cols] = y.astype(BF16).reshape(group, rows, cw)
            return carry

        lax.fori_loop(0, nc // group, block, 0)
        own[j] = tmp[c]

    def edge_send(j):
        for far in range(nc - 1):
            @pl.when(c == 0)
            def _(far=far):
                go_right(j, nc - 1 - far).start()

            @pl.when(c == nc - 1)
            def _(far=far):
                go_left(j, far).start()

    def reduce_right(j):
        for far in range(nc - 2):
            dest = nc - 1 - far

            @pl.when(c < dest)
            def _(dest=dest):
                go_right(j, dest).wait_recv()
                part[j, dest] = (part[j, dest].astype(F32) + landing[j, dest + 1].astype(F32)).astype(BF16)
                go_right(j, dest).start()

    def reduce_left(j):
        for dest in range(nc - 2):
            @pl.when(c > dest)
            def _(dest=dest):
                go_left(j, dest).wait_recv()
                part[j, dest] = (part[j, dest].astype(F32) + landing[j, dest].astype(F32)).astype(BF16)
                go_left(j, dest).start()

    def gather_copy(j, block, direction):
        to_c = lax.rem(c + 1, nc) if direction == 0 else lax.rem(c + nc - 1, nc)
        return remote(
            gathered.at[j, block], gathered.at[j, block], ag_send.at[direction, j, block],
            ag_recv.at[j, block], to_c, h,
        )

    loss_acc[...] = jnp.zeros_like(loss_acc)
    def keep_of(j, block):
        return wide_keep[block, :, cols_of(j)].astype(F32)

    def derive(j, i):
        gate = gathered[j, i, :, 0:cw].astype(F32)
        up = gathered[j, i, :, cw : 2 * cw].astype(F32)
        lifted = jnp.maximum(gate, 0.0)
        squared = lifted * lifted
        act = squared * up
        differ = act - feats[i, :, cols_of(j)].astype(F32)
        grad_act = keep_of(j, i) * differ
        at = lax.rem(j, depth)
        terms[at, 0, i] = act.astype(BF16)
        terms[at, 1, i] = (grad_act * up * 2.0 * lifted).astype(BF16)
        terms[at, 2, i] = (grad_act * squared).astype(BF16)

    def features(j):
        @pl.when(c > 0)
        def _():
            go_right(j, c).wait_recv()
            own[j] = own[j] + landing[j, c + 1].astype(F32)

        @pl.when(c < nc - 1)
        def _():
            go_left(j, c).wait_recv()
            own[j] = own[j] + landing[j, c].astype(F32)

        gate = own[j, :, 0:cw]
        up = own[j, :, cw : 2 * cw]
        lifted = jnp.maximum(gate, 0.0)
        squared = lifted * lifted
        act = squared * up
        differ = act - feats_ref[:, cols_of(j)].astype(F32)
        loss_acc[...] += keep_of(j, c) * differ * differ
        gathered[j, c] = own[j].astype(BF16)

        @pl.when(c < nc - 1)
        def _():
            gather_copy(j, c, 0).start()

        @pl.when(c > 0)
        def _():
            gather_copy(j, c, 1).start()

    def forward(j, far):
        @pl.when(c >= far)
        def _():
            block = lax.rem(c - far + nc, nc)
            gather_copy(j, block, 0).wait_recv()

            @pl.when(c < nc - 1)
            def _():
                gather_copy(j, block, 0).start()

        @pl.when(c + far < nc)
        def _():
            block = lax.rem(c + far, nc)
            gather_copy(j, block, 1).wait_recv()

            @pl.when(c > 0)
            def _():
                gather_copy(j, block, 1).start()

    def derive_far(j, far):
        @pl.when(c >= far)
        def _():
            derive(j, lax.rem(c - far + nc, nc))

        @pl.when(c + far < nc)
        def _():
            derive(j, lax.rem(c + far, nc))

    contract = (((1,), (1,)), ((), ()))
    acc_down[...] = jnp.zeros_like(acc_down)
    acc_grad[...] = jnp.zeros_like(acc_grad)

    def accumulate(j):
        def block(i, carry):
            at = pl.ds(i * group, group)

            def rows_of(k):
                return terms[lax.rem(j, depth), k, at].reshape(group * rows, cw)

            down = jnp.dot(rows_of(0), wd[cols_of(j), :], preferred_element_type=F32)
            acc_down[at] += down.reshape(group, rows, dc)
            grad = lax.dot_general(
                rows_of(1), wg[:, cols_of(j)], contract, preferred_element_type=F32
            ) + lax.dot_general(rows_of(2), wu[:, cols_of(j)], contract, preferred_element_type=F32)
            acc_grad[at] += grad.reshape(group, rows, dc)
            return carry

        lax.fori_loop(0, nc // group, block, 0)

    ahead = 2
    feature_lag = max(nc - 2, 1)
    inside = (c > 0) & (c < nc - 1)

    def step(i, carry):
        def when(lag, body, also=True):
            j = i - lag

            @pl.when((j >= 0) & (j < chunks) & also)
            def _():
                body(j)

        when(c - 1, reduce_right, inside)
        when(nc - 2 - c, reduce_left, inside)
        when(feature_lag, features)
        for far in range(1, nc):
            when(feature_lag + far, functools.partial(forward, far=far))
        when(-1, edge_send)

        @pl.when(i < nc - 2)
        def _():
            feats_forward(i + 2)

        when(-ahead, multiply)
        when(feature_lag, lambda j: derive(j, c))
        for far in range(1, nc):
            when(feature_lag + far, functools.partial(derive_far, far=far))
        when(feature_lag + nc - 1, accumulate)
        return carry

    multiply(0)
    edge_send(0)
    multiply(1)
    lax.fori_loop(0, chunks + feature_lag + nc - 1, step, 0)

    loss_part = jnp.sum(jnp.sum(loss_acc[...], axis=1, keepdims=True), axis=0, keepdims=True)
    count_part = jnp.sum(
        jnp.sum(keep_ref[...].astype(F32), axis=1, keepdims=True), axis=0, keepdims=True
    ) * TILE
    line = lax.broadcasted_iota(jnp.int32, (8, TILE), 0)
    loss_head[h] = jnp.where(line == 0, loss_part, count_part)
    peers(lambda o: remote(loss_head.at[h], loss_head.at[h], lh_send.at[o], lh_recv.at[h], c, o).start())

    def pair_copy(p, k, slot):
        return remote(
            sums.at[p, k], pair_in.at[slot, k], p_send.at[p, k], p_recv.at[slot, k],
            c, my_head * npair + p,
        )

    for k in range(nc):
        for p in range(npair):
            for g in range(nhead):
                o = g * npair + p
                sums[p, k, g, 0] = acc_down[k, o * sub : (o + 1) * sub].astype(BF16)
                sums[p, k, g, 1] = acc_grad[k, o * sub : (o + 1) * sub].astype(BF16)
        others(npair, my_pair, lambda p: pair_copy(p, k, my_pair).start())

    def head_copy(g, k, slot):
        return remote(
            sums.at[my_pair, k, g], head_in.at[slot, k], h_send.at[g, k], h_recv.at[slot, k],
            c, g * npair + my_pair,
        )

    for k in range(nc):
        def add_pair(p):
            pair_copy(p, k, p).wait_recv()
            sums[my_pair, k] = (
                sums[my_pair, k].astype(F32) + pair_in[p, k].astype(F32)
            ).astype(BF16)

        others(npair, my_pair, add_pair)
        others(nhead, my_head, lambda g: head_copy(g, k, my_head).start())

    peers(lambda o: remote(loss_head.at[o], loss_head.at[o], lh_send.at[o], lh_recv.at[o], c, o).wait_recv())
    head_total = loss_head[0]
    for other in range(1, nh):
        head_total = head_total + loss_head[other]
    loss_ctx[c] = head_total

    def loss_copy(block, to_c):
        return remote(
            loss_ctx.at[block], loss_ctx.at[block], lc_send.at[to_c], lc_recv.at[block], to_c, h
        )

    for other in range(nc):
        @pl.when(other != c)
        def _(other=other):
            loss_copy(c, other).start()

    to_h = c // nb
    slot = lax.rem(c, nb) if nb > 1 else 0

    def final_copy(block):
        return remote(
            sums.at[my_pair, block, my_head], final.at[slot, h], f_send.at[block],
            f_recv.at[slot, h], block, to_h,
        )

    for block in range(nc):
        def add_head(g):
            head_copy(g, block, g).wait_recv()
            sums[my_pair, block, my_head] = (
                sums[my_pair, block, my_head].astype(F32) + head_in[g, block].astype(F32)
            ).astype(BF16)

        others(nhead, my_head, add_head)
        mine = (block == c) & (to_h == h)

        @pl.when(jnp.logical_not(mine))
        def _(block=block):
            final_copy(block).start()

        @pl.when(mine)
        def _(block=block):
            final[slot, h] = sums[my_pair, block, my_head]

    for b in range(nb):
        for other in range(nh):
            from_c = h * nb + b

            @pl.when((from_c != c) | (other != h))
            def _(b=b, other=other, from_c=from_c):
                remote(
                    final.at[b, other], final.at[b, other], f_send.at[0], f_recv.at[b, other],
                    from_c, other,
                ).wait_recv()

    inner_part = jnp.zeros((rows, 1), F32)
    for b in range(nb):
        cols = slice(b * dc, (b + 1) * dc)
        down = final[b, :, 0].reshape(rows, dc).astype(F32)
        out_ref[:, cols] = (resid[:, cols].astype(F32) + down).astype(BF16)
        grad_norm = final[b, :, 1].reshape(rows, dc).astype(F32)
        inner_part += jnp.sum(
            gain_own[:, cols] * grad_norm * resid[:, cols].astype(F32), axis=1, keepdims=True
        )
    inner[h] = jnp.broadcast_to(inner_part, (rows, TILE))
    inner_sum = exchange(inner, in_send, in_recv)[:, :1]
    rms = jnp.sqrt(
        functools.reduce(lambda a, b: a + b, [squares[o] for o in range(nh)])[:, :1] / width + 1e-05
    )
    scale = inner_sum / (width * (rms * rms * rms))
    for b in range(nb):
        cols = slice(b * dc, (b + 1) * dc)
        grad_norm = final[b, :, 1].reshape(rows, dc).astype(F32)
        grad_ref[:, cols] = (
            gain_own[:, cols] * grad_norm / rms - resid[:, cols].astype(F32) * scale
        )

    for other in range(nc):
        @pl.when(other != c)
        def _(other=other):
            loss_copy(other, other).wait_recv()
    total = loss_ctx[0]
    for other in range(1, nc):
        total = total + loss_ctx[other]
    loss_ref[...] = total[0:1, 0:1] / total[1:2, 0:1]

    for other in range(nc):
        @pl.when(other > c)
        def _(other=other):
            for copy in kv_copies(c, other):
                copy.wait_send()

        @pl.when(other != c)
        def _(other=other):
            loss_copy(c, other).wait_send()

    exchange_end(squares, sq_send, sq_recv)
    exchange_end(inner, in_send, in_recv)
    for b in range(nb):
        for other in range(nh):
            @pl.when((h * nb + b != c) | (other != h))
            def _(b=b, other=other):
                hop_one(b, other).wait_send()
    for block in range(nc):
        others(nhead, my_head, lambda g: to_head(block, h, g).wait_send())
        for g in range(nhead):
            others(npair, my_pair, lambda p: to_mate(block, g * npair + my_pair, p).wait_send())

        @pl.when((block <= c) & (c < nc - 1))
        def _(block=block):
            feats_copy(block, 0).wait_send()

        @pl.when((block >= c) & (c > 0))
        def _(block=block):
            feats_copy(block, 1).wait_send()

    others(nc, c, lambda o: keep_copy(c, o).wait_send())
    peers(lambda o: remote(loss_head.at[h], loss_head.at[h], lh_send.at[o], lh_recv.at[h], c, o).wait_send())

    def drain(j, carry):
        for block in range(nc):
            @pl.when(block > c)
            def _(block=block):
                go_right(j, block).wait_send()

            @pl.when(block < c)
            def _(block=block):
                go_left(j, block).wait_send()

            @pl.when((block <= c) & (c < nc - 1))
            def _(block=block):
                gather_copy(j, block, 0).wait_send()

            @pl.when((block >= c) & (c > 0))
            def _(block=block):
                gather_copy(j, block, 1).wait_send()

        return carry

    lax.fori_loop(0, chunks, drain, 0)
    for k in range(nc):
        others(npair, my_pair, lambda p: pair_copy(p, k, my_pair).wait_send())
        others(nhead, my_head, lambda g: head_copy(g, k, my_head).wait_send())
    for block in range(nc):
        @pl.when((block != c) | (to_h != h))
        def _(block=block):
            final_copy(block).wait_send()


def local(
    student_query, teacher_keys, teacher_values, band_span, residual_in, norm_gain,
    w_gate, w_up, w_down, teacher_feats, keep_tiles,
):
    nc, nhead, npair = (lax.axis_size(a) for a in ("ctx", "head", "pair"))
    nh = nhead * npair
    nb = nc // nh
    rows, own_cols = residual_in.shape
    sub = rows // nh
    dc, ff = w_gate.shape
    chunks = CHUNKS
    cw = ff // chunks
    kv = teacher_keys.shape[1]
    vmem = pl.BlockSpec(memory_space=pltpu.VMEM)
    hbm = pl.BlockSpec(memory_space=pl.ANY)
    dma = lambda *shape: pltpu.SemaphoreType.DMA(shape)
    kernel = functools.partial(layer_kernel, nc, nhead, npair, chunks)
    layer_out, loss, grad = pl.pallas_call(
        kernel,
        out_shape=(
            jax.ShapeDtypeStruct((rows, own_cols), BF16),
            jax.ShapeDtypeStruct((1, 1), F32),
            jax.ShapeDtypeStruct((rows, own_cols), F32),
        ),
        in_specs=[vmem] * 6 + [hbm] * 3 + [vmem] * 2,
        out_specs=(vmem, vmem, vmem),
        scratch_shapes=[
            pltpu.VMEM((dc, ff), BF16),
            pltpu.VMEM((dc, ff), BF16),
            pltpu.VMEM((ff, dc), BF16),
            pltpu.VMEM((nc, rows, kv), BF16),
            pltpu.VMEM((nc, rows, kv), BF16),
            pltpu.VMEM((rows, own_cols), BF16),
            pltpu.VMEM((nh, rows, TILE), F32),
            pltpu.VMEM((nb, nh, sub, dc), BF16),
            pltpu.VMEM((nc, nh, sub, dc), BF16),
            pltpu.VMEM((nc, rows, 2 * cw), F32),
            pltpu.VMEM((chunks, nc, rows, 2 * cw), BF16),
            pltpu.VMEM((chunks, nc + 1, rows, 2 * cw), BF16),
            pltpu.VMEM((chunks, rows, 2 * cw), F32),
            pltpu.VMEM((chunks, nc, rows, 2 * cw), BF16),
            pltpu.VMEM((nc, rows, dc), F32),
            pltpu.VMEM((nc, rows, dc), F32),
            pltpu.VMEM((nc, rows, ff), BF16),
            pltpu.VMEM((nc, ff // TILE, rows), jnp.int32),
            pltpu.VMEM((nc, rows, ff), BF16),
            pltpu.VMEM((min(chunks, nc), 3, nc, rows, cw), BF16),
            pltpu.VMEM((npair, nc, nhead, 2, sub, dc), BF16),
            pltpu.VMEM((npair, nc, nhead, 2, sub, dc), BF16),
            pltpu.VMEM((nhead, nc, 2, sub, dc), BF16),
            pltpu.VMEM((nb, nh, 2, sub, dc), BF16),
            pltpu.VMEM((nh, rows, TILE), F32),
            pltpu.VMEM((nh, 8, TILE), F32),
            pltpu.VMEM((nc, 8, TILE), F32),
            pltpu.VMEM((rows, cw), F32),
            dma(3),
            dma(2, nc), dma(2, nc),
            dma(nh), dma(nh),
            dma(nb, nh), dma(nc),
            dma(nhead, nc), dma(npair, nh, nc), dma(nh, nc),
            dma(2, nc), dma(nc),
            dma(nc), dma(nc),
            dma(chunks, nc), dma(chunks, nc), dma(chunks, nc),
            dma(2, chunks, nc), dma(chunks, nc),
            dma(npair, nc), dma(npair, nc),
            dma(nhead, nc), dma(nhead, nc),
            dma(nc), dma(nb, nh),
            dma(nh), dma(nh),
            dma(nh), dma(nh),
            dma(nc), dma(nc),
        ],
        compiler_params=pltpu.CompilerParams(
            collective_id=0, has_side_effects=True, vmem_limit_bytes=60 * 1024 * 1024
        ),
        cost_estimate=pl.CostEstimate(
            flops=10 * nc * rows * dc * ff, bytes_accessed=6 * dc * ff, transcendentals=0
        ),
    )(
        student_query, teacher_keys, teacher_values, band_span.reshape(1, rows), residual_in,
        norm_gain.reshape(1, -1), w_gate, w_up, w_down, teacher_feats, keep_tiles.T,
    )
    return (layer_out, loss.reshape(1), grad)


def solution(mesh):
    in_specs = (
        P(("groups", "ctx"), ("head", "pair")),
        P(("groups", "ctx"), ("head", "pair")),
        P(("groups", "ctx"), ("head", "pair")),
        P(("groups", "ctx")),
        P(("groups", "ctx"), ("head", "pair")),
        P(),
        P("ctx", ("head", "pair")),
        P("ctx", ("head", "pair")),
        P(("head", "pair"), "ctx"),
        P(("groups", "ctx"), ("head", "pair")),
        P(("groups", "ctx"), ("head", "pair")),
    )
    out_specs = (
        P(("groups", "ctx"), ("head", "pair")),
        P("groups"),
        P(("groups", "ctx"), ("head", "pair")),
    )
    return jax.shard_map(local, mesh=mesh, in_specs=in_specs, out_specs=out_specs, check_vma=False)
```
